512 devices in a mesh: band: 64 (over y, z), fld: 8 (over x, core).
Axes of the slice: x: 4, y: 8, z: 8, core: 2. Of those that a mesh axis runs over, the one named last changes fastest.
Arguments:
- grid: bfloat16 [8, 64, 256, 2596], P('fld', 'band'), may hold values from -6 to 6
- pair_ids: int32 [8, 64], P('fld', 'band'), may hold values from 0 to 319, as said below
- trims: int32 [8, 64, 2], P('fld', 'band'), may hold values from 0 to 79
- weights: float32 [8, 64, 2], P('fld', 'band'), may hold values from 100 to 1000
- wavenumbers: int32 [640], replicated, may hold values from 0 to 639, as said below
- legendre: bfloat16 [320, 1024, 641], P('band', 'fld'), may hold values from -0.03125 to 0.03125
- damping: float32 [640], replicated, may hold values from 0.1 to 1
Outputs:
- spectrum: bfloat16 [320, 2, 256, 641], P('band', None, 'fld')
- restored: bfloat16 [8, 64, 256, 2596], P('fld', 'band')
The draws below stay inside these ranges and needn't reach their ends.
Inputs may be any that keep to these rules, and one draw needn't show every extreme that they name: `pair_ids`: pair index i of each slot; its cycles have 20 + 4 i and 20 + 4 (639 - i) points. `wavenumbers`: entries 2 q and 2 q + 1 sum to 639; each wavenumber appears once.
All inputs are finite; a program needn't handle non-finite values.
Results may differ from the reference program's by a relative error of at most 0.02.
Values may be sent and summed in bfloat16 or wider, within the bound.
No kernel may reach another device: no remote copies, remote signals or barrier semaphores. Data moves between devices by JAX's collectives and lax.ppermute only.
A program may use at most 64 MiB of HBM per device.

```python
import math
import jax
import jax.numpy as jnp
from jax import lax

M = 639
FIELDS = 256
WPAIRS = 320
DEG_PAIR = 641
PAIR_LEN = 2596
CYCLE_GROUPS = 8
GROUP_PAIRS = 64
CYCLES = 1024


def draw_pair_ids(key, part):
    key = jax.random.fold_in(key, 11)
    number_of_slots = CYCLE_GROUPS * GROUP_PAIRS
    spread = jnp.arange(number_of_slots, dtype=jnp.int32) * (WPAIRS - 1) // max(number_of_slots - 1, 1)
    return jax.random.permutation(key, spread).reshape(CYCLE_GROUPS, GROUP_PAIRS).astype(jnp.int32)


def draw_wavenumbers(key, part):
    key = jax.random.fold_in(key, 23)
    order_key, flip_key = jax.random.split(key)
    lowest = jax.random.permutation(order_key, WPAIRS).astype(jnp.int32)
    flipped = jax.random.randint(flip_key, (WPAIRS,), 0, 2)
    leading = jnp.where(flipped == 1, M - lowest, lowest)
    return jnp.stack([leading, M - leading], axis=1).reshape(M + 1).astype(jnp.int32)


def with_ends(values, stream_key, smallest, top_value):
    place = [jax.random.randint(jax.random.fold_in(stream_key, axis), (), 0, length) for axis, length in enumerate(values.shape)]
    longest = values.shape.index(max(values.shape))
    next_to = place[:longest] + [(place[longest] + 1) % values.shape[longest]] + place[longest + 1:]
    return values.at[tuple(place)].set(smallest).at[tuple(next_to)].set(top_value)


def steps_of(key, dims, cuts, low, high):
    level = 1.0
    for axis_at, blocks in cuts:
        steps = jax.random.uniform(jax.random.fold_in(jax.random.fold_in(key, 6), axis_at), (blocks,), jnp.float32, low / len(cuts), high / len(cuts))
        level = level * jnp.repeat(jnp.exp(steps), dims[axis_at] // blocks).reshape((-1,) + (1,) * (len(dims) - 1 - axis_at))
    return level


def scatter_about(rng, extent, deviation, reach, cuts=(), kind=jnp.bfloat16):
    result = deviation * jax.random.normal(rng, extent, jnp.float32)
    if cuts:
        result = result * steps_of(rng, extent, cuts, -0.22, 0.18)
    return jnp.clip(result, -reach, reach).astype(kind)


def setup_inputs(seed: int = 0) -> dict:
    arg_keys = jax.random.split(jax.random.key(seed), 8)
    return {
        "grid": scatter_about(arg_keys[0], (CYCLE_GROUPS, GROUP_PAIRS, FIELDS, PAIR_LEN), 1.0, 6.0, ((0, 8), (1, 64))),
        "pair_ids": draw_pair_ids(jax.random.fold_in(arg_keys[7], 71), 0),
        "trims": with_ends(jax.random.randint(arg_keys[2], (CYCLE_GROUPS, GROUP_PAIRS, 2), 0, M // 8 + 1), jax.random.fold_in(arg_keys[2], 1), 0, (M // 8 + 1) - 1).astype(jnp.int32),
        "weights": jnp.clip(jnp.exp(math.log(1000.0) - 2.3025851 * jax.random.uniform(arg_keys[3], (CYCLE_GROUPS, GROUP_PAIRS, 2), jnp.float32) ** steps_of(arg_keys[3], (CYCLE_GROUPS, GROUP_PAIRS, 2), ((0, 8), (1, 64)), -0.2, 0.2)), 100.0, 1000.0),
        "wavenumbers": draw_wavenumbers(jax.random.fold_in(arg_keys[7], 71), 0),
        "legendre": scatter_about(arg_keys[5], (WPAIRS, CYCLES, DEG_PAIR), (64 * (M + 1)) ** -0.5, 0.03125, ((0, 64), (1, 8))),
        "damping": jnp.clip(jnp.exp(jax.random.uniform(arg_keys[6], (M + 1,), jnp.float32, math.log(0.1), math.log(1.0))), 0.1, 1.0),
    }


TWO_PI = 6.283185307179586


def pair_table(first_count, limit_pair, wavenumbers, length):
    row_index = jnp.arange(length, dtype=jnp.int32)
    in_second = row_index >= first_count
    local_index = jnp.where(in_second, row_index - first_count, row_index)
    cycle_count = jnp.where(in_second, length - first_count, first_count)
    cycle_limit = jnp.where(in_second, limit_pair[1], limit_pair[0])
    residue = (local_index[:, None] * wavenumbers[None, :]) % cycle_count[:, None]
    angles = TWO_PI * (residue.astype(jnp.float32) / cycle_count[:, None].astype(jnp.float32))
    kept_mask = wavenumbers[None, :] <= cycle_limit[:, None]
    cosine = jnp.where(kept_mask, jnp.cos(angles), 0.0)
    minus_sine = jnp.where(kept_mask, -jnp.sin(angles), 0.0)
    return jnp.concatenate([cosine, minus_sine], axis=1).astype(jnp.bfloat16)


def split_cycles(cycle_block, first_count):
    in_second = jnp.arange(cycle_block.shape[1], dtype=jnp.int32) >= first_count
    zeros_block = jnp.zeros_like(cycle_block)
    return jnp.stack([jnp.where(in_second[None, :], zeros_block, cycle_block),
                      jnp.where(in_second[None, :], cycle_block, zeros_block)])


def reference(grid, pair_ids, trims, weights, wavenumbers, legendre, damping):
    groups, pairs_each, fields, length = grid.shape
    number_of_slots = groups * pairs_each
    columns = wavenumbers.shape[0]
    highest = columns - 1
    packed = legendre.shape[2]
    blocks_per_cycle = grid.reshape(number_of_slots, fields, length)
    leading_counts = 20 + 4 * pair_ids.reshape(number_of_slots)
    degree_counts = jnp.stack([leading_counts, length - leading_counts], axis=1)
    degree_limits = jnp.maximum(jnp.minimum(highest, degree_counts // 2 - 1) - trims.reshape(number_of_slots, 2), 0)
    degree_scales = weights.reshape(number_of_slots, 2) / degree_counts.astype(jnp.float32)

    def forward_inverse_pair(member):
        cycle_block, first_count, limit_pair, scaling = member
        twiddles = pair_table(first_count, limit_pair, wavenumbers, length)
        stacked = split_cycles(cycle_block, first_count).reshape(2 * fields, length)
        raw_sums = lax.dot_general(twiddles, stacked, (((0,), (1,)), ((), ())), preferred_element_type=jnp.float32)
        coefficients = raw_sums.reshape(2, columns, 2, fields) * scaling[None, None, :, None]
        return coefficients.astype(jnp.bfloat16)

    fourier_modes = lax.map(forward_inverse_pair, (blocks_per_cycle, leading_counts, degree_limits, degree_scales))
    by_column = fourier_modes.transpose(2, 0, 3, 1, 4).reshape(columns, 2 * number_of_slots, 2, fields)
    packed_index = jnp.arange(packed, dtype=jnp.int32)

    def forward_wave(wave_pair):
        wave_rows = lax.dynamic_slice_in_dim(by_column, 2 * wave_pair, 2, 0).astype(jnp.float32)
        opening = lax.dynamic_index_in_dim(wavenumbers, 2 * wave_pair, 0, keepdims=False)
        first_part = packed_index < highest + 1 - opening
        matrix = lax.dynamic_index_in_dim(legendre, wave_pair, 0, keepdims=False).astype(jnp.float32)
        grouped_rows = wave_rows.reshape(2, groups, -1, 2, fields)
        grouped_matrix = matrix.reshape(groups, -1, packed)
        partial_value = jnp.einsum('htrpf,trk->thpfk', grouped_rows, grouped_matrix)
        partial_value = lax.optimization_barrier(partial_value.astype(jnp.bfloat16)).astype(jnp.float32)
        summed = jnp.sum(partial_value, axis=0)
        chosen = jnp.where(first_part, summed[0], summed[1])
        degree = jnp.where(first_part, opening + packed_index, packed_index - 1)
        return (chosen * damping[degree]).astype(jnp.bfloat16)

    wave_pairs = jnp.arange(columns // 2, dtype=jnp.int32)
    spectrum = lax.map(forward_wave, wave_pairs)

    def inverse_wave(wave_pair):
        coeffs = lax.dynamic_index_in_dim(spectrum, wave_pair, 0, keepdims=False)
        opening = lax.dynamic_index_in_dim(wavenumbers, 2 * wave_pair, 0, keepdims=False)
        first_part = packed_index < highest + 1 - opening
        nothing = jnp.zeros_like(coeffs)
        split_parts = jnp.stack([jnp.where(first_part, coeffs, nothing),
                                 jnp.where(first_part, nothing, coeffs)]).astype(jnp.float32)
        matrix = lax.dynamic_index_in_dim(legendre, wave_pair, 0, keepdims=False).astype(jnp.float32)
        rebuilt = jnp.einsum('hpfk,rk->hrpf', split_parts, matrix)
        return rebuilt.astype(jnp.bfloat16)

    returned = lax.map(inverse_wave, wave_pairs).reshape(columns, number_of_slots, 2, 2, fields)
    per_pair = returned.transpose(1, 3, 0, 2, 4)
    doubling = jnp.where(wavenumbers == 0, 1.0, 2.0).astype(jnp.bfloat16)

    def inverse_pair(member):
        coefficients, first_count, limit_pair = member
        twiddles = pair_table(first_count, limit_pair, wavenumbers, length)
        scaled = (coefficients * doubling[None, :, None, None]).reshape(2 * columns, 2 * fields)
        rows_out = lax.dot_general(scaled, twiddles, (((0,), (1,)), ((), ())), preferred_element_type=jnp.float32)
        rows_out = rows_out.reshape(2, fields, length)
        in_second = jnp.arange(length, dtype=jnp.int32) >= first_count
        return jnp.where(in_second[None, :], rows_out[1], rows_out[0]).astype(jnp.bfloat16)

    restored = lax.map(inverse_pair, (per_pair, leading_counts, degree_limits))
    return spectrum, restored.reshape(groups, pairs_each, fields, length)
```

```python
import functools

import jax
import jax.numpy as jnp
from jax import lax
from jax.experimental import pallas as pl
from jax.experimental.pallas import tpu as pltpu
from jax.sharding import PartitionSpec as P

PI = 3.141592653589793
LANES = 128
BLOCK = 256
STRIP = 64
VMEM_BYTES = 40 * 1024 * 1024
CHUNKS = ((0, 5),)


def unit_circle(waves, points, count):
    inverse = 1.0 / count
    product = waves * points
    residue = product - jnp.round(product * inverse) * count
    half = residue * (inverse * PI)
    square = half * half
    sine = 1.0 / 6227020800.0
    for term in (-1.0 / 39916800.0, 1.0 / 362880.0, -1.0 / 5040.0, 1.0 / 120.0, -1.0 / 6.0, 1.0):
        sine = sine * square + term
    sine = sine * half
    cosine = 1.0 / 479001600.0
    for term in (-1.0 / 3628800.0, 1.0 / 40320.0, -1.0 / 720.0, 1.0 / 24.0, -0.5, 1.0):
        cosine = cosine * square + term
    return cosine * cosine - sine * sine, -2.0 * sine * cosine


def turn(state, step):
    cosine, sine = state
    return cosine * step[0] - sine * step[1], sine * step[0] + cosine * step[1]


def cycle_facts(length, highest, pair_ids, trims):
    first = 20 + 4 * pair_ids[0, 0]
    counts = (first, length - first)
    limits = [
        jnp.maximum(jnp.minimum(highest, count // 2 - 1) - trims[0, 0, cycle], 0)
        for cycle, count in enumerate(counts)
    ]
    return first, [c.astype(jnp.float32) for c in counts], [l.astype(jnp.float32) for l in limits]


def fill_table(axis, chosen, step_waves, facts, blocks, write):
    first, counts, limits = facts
    shape = chosen.shape
    lane = lax.broadcasted_iota(jnp.int32, shape, axis)
    straddle = first // LANES

    def begin(cycle, offset):
        state = unit_circle(chosen, (lane + offset).astype(jnp.float32), counts[cycle])
        kept = chosen <= limits[cycle]
        return tuple(jnp.where(kept, part, 0.0) for part in state)

    steps = step_waves(counts)

    def advance(cycle):
        def body(block, state):
            write(block, state)
            return turn(state, steps[cycle])

        return body

    state = lax.fori_loop(0, straddle, advance(0), begin(0, 0))
    offset = straddle * LANES - first
    later = begin(1, offset)
    before = lane + offset < 0
    write(straddle, tuple(jnp.where(before, old, new) for old, new in zip(state, later)))
    lax.fori_loop(straddle + 1, blocks, advance(1), turn(later, steps[1]))


def forward_kernel(highest, bands, pair_ids, trims, weights, waves, grid, packed, table, totals, columns, rows):
    length, fields = grid.shape
    width = waves.shape[1]
    quarter = width // 2
    facts = cycle_facts(length, highest, pair_ids, trims)
    first, counts, _ = facts
    blocks = -(-length // LANES)
    columns[...] = jnp.broadcast_to(waves[...].astype(jnp.float32), (LANES, width)).T

    for strip in range(width // STRIP):
        chosen = columns[strip * STRIP:(strip + 1) * STRIP, :]

        def step_waves(counts):
            cycle_lane = lax.broadcasted_iota(jnp.int32, chosen.shape, 1)
            count = jnp.where(cycle_lane == 0, counts[0], counts[1])
            cosine, sine = unit_circle(chosen, float(LANES), count)
            return [
                tuple(jnp.broadcast_to(part[:, c:c + 1], chosen.shape) for part in (cosine, sine))
                for c in range(2)
            ]

        def write(block, state):
            for part in range(2):
                table[
                    part * width + strip * STRIP:part * width + (strip + 1) * STRIP,
                    pl.ds(pl.multiple_of(block * LANES, LANES), LANES),
                ] = state[part].astype(jnp.bfloat16)

        fill_table(1, chosen, step_waves, facts, blocks, write)

    full = length // BLOCK
    straddle = first // BLOCK
    position = lax.broadcasted_iota(jnp.int32, (BLOCK, fields), 0)

    def product(start, size, data):
        return jnp.dot(table[:, pl.ds(start, size)], data, preferred_element_type=jnp.float32)

    def data_of(block):
        return grid[pl.ds(pl.multiple_of(block * BLOCK, BLOCK), BLOCK), :]

    def add(cycle):
        def body(block, carry):
            totals[cycle] += product(pl.multiple_of(block * BLOCK, BLOCK), BLOCK, data_of(block))
            return carry

        return body

    data = data_of(straddle)
    before = position + straddle * BLOCK < first
    nothing = jnp.zeros_like(data)
    start = pl.multiple_of(straddle * BLOCK, BLOCK)
    totals[0] = product(start, BLOCK, jnp.where(before, data, nothing))
    totals[1] = product(start, BLOCK, jnp.where(before, nothing, data))
    lax.fori_loop(0, straddle, add(0), 0)
    lax.fori_loop(straddle + 1, full, add(1), 0)
    totals[1] += product(full * BLOCK, length - full * BLOCK, grid[full * BLOCK:, :])

    share = LANES // 4
    for group in range(fields // share):
        lanes = slice(group * share, (group + 1) * share)
        for cycle in range(2):
            scale = jnp.full((1, LANES), weights[0, 0, cycle]) / counts[cycle]
            joined = jnp.concatenate(
                [totals[cycle, part * quarter:(part + 1) * quarter, lanes] for part in (0, 2, 1, 3)], axis=1
            )
            rows[pl.ds(cycle, quarter, stride=2), :] = joined * scale
        packed[group] = rows[...].astype(jnp.bfloat16)


def table_kernel(length, highest, pair_ids, trims, *refs):
    *waves, table = refs
    facts = cycle_facts(length, highest, pair_ids, trims)
    blocks = -(-length // LANES)
    base = 0
    for chunk in waves:
        width = chunk.shape[1]
        for tile in range(width // LANES):
            row = chunk[:, tile * LANES:(tile + 1) * LANES].astype(jnp.float32)
            chosen = jnp.broadcast_to(row, (LANES, LANES))

            def step_waves(counts):
                wide = jnp.broadcast_to(row, (8, LANES))
                return [
                    tuple(part[:1] for part in unit_circle(wide, float(LANES), count)) for count in counts
                ]

            def write(block, state):
                for part in range(2):
                    left = base + part * width + tile * LANES
                    table[pl.ds(pl.multiple_of(block * LANES, LANES), LANES), left:left + LANES] = (
                        state[part].astype(jnp.bfloat16)
                    )

            fill_table(0, chosen, step_waves, facts, blocks, write)
        base += 2 * width


def legendre_kernel(start, highest, band, wavenumbers, values, legendre, damping, *refs):
    spectrum, rebuilt = refs[-2:]
    groups, _, degrees, each = legendre.shape
    matrix = jnp.concatenate([legendre[group, 0] for group in range(groups)], axis=1)
    sums = lax.dot_general(
        values[0].T, matrix, (((1,), (1,)), ((), ())), preferred_element_type=jnp.float32
    )
    fields = sums.shape[0] // 2
    pair = band[0] + start + pl.program_id(0)
    first_wave = wavenumbers[2 * pair]
    second_wave = wavenumbers[2 * pair + 1]
    width = damping.shape[1]
    degree = lax.broadcasted_iota(jnp.int32, (1, width), 1)
    kept = degree < highest + 1 - first_wave
    upper = pltpu.roll(damping[...], lax.rem(width - first_wave, width), 1)
    lower = pltpu.roll(damping[...], 1, 1)
    factor = jnp.where(kept, upper[:1], lower[:1])[:, :degrees]
    head = jnp.broadcast_to(kept[:, :degrees], (fields, degrees))
    filtered = (jnp.where(head, sums[:fields], sums[fields:]) * factor).astype(jnp.bfloat16)
    spectrum[0] = filtered
    nothing = jnp.zeros_like(filtered)
    parts = jnp.concatenate([jnp.where(head, filtered, nothing), jnp.where(head, nothing, filtered)], axis=0)
    products = jnp.dot(parts, matrix, preferred_element_type=jnp.float32)
    row = lax.broadcasted_iota(jnp.int32, products.shape, 0)
    wave = jnp.where(row < fields, first_wave, second_wave)
    doubled = products * jnp.where(wave == 0, 1.0, 2.0)
    rebuilt[0] = doubled.astype(jnp.bfloat16).T


def inverse_kernel(chunks, pair_ids, *refs):
    values = refs[:chunks]
    table, restored, rows, factors = refs[chunks:]
    block = pl.program_id(0)
    first = 20 + 4 * pair_ids[0, 0]
    share = LANES // 4

    @pl.when(block == 0)
    def _():
        base = 0
        for chunk in values:
            groups, height, _ = chunk.shape
            quarter = height // 2
            for side in range(groups // 4):
                for near in range(4):
                    rows[near, :height] = chunk[4 * side + near].astype(jnp.float32)
                for cycle in range(2):
                    turned = [
                        rows[near, pl.ds(cycle, quarter, stride=2), :].astype(jnp.bfloat16) for near in range(4)
                    ]
                    for part in range(4):
                        source = (0, 2, 1, 3)[part] * share
                        factors[
                            cycle,
                            base + part * quarter:base + (part + 1) * quarter,
                            side * LANES:(side + 1) * LANES,
                        ] = jnp.concatenate([one[:, source:source + share] for one in turned], axis=1)
            base += 4 * quarter

    def product(cycle):
        return jnp.dot(table[...], factors[cycle], preferred_element_type=jnp.float32)

    start = block * BLOCK
    end = start + BLOCK

    @pl.when(end <= first)
    def _():
        restored[...] = product(0).astype(jnp.bfloat16)

    @pl.when(start >= first)
    def _():
        restored[...] = product(1).astype(jnp.bfloat16)

    @pl.when((start < first) & (end > first))
    def _():
        position = start + lax.broadcasted_iota(jnp.int32, restored.shape, 0)
        restored[...] = jnp.where(position < first, product(0), product(1)).astype(jnp.bfloat16)


SMEM = pl.BlockSpec(memory_space=pltpu.SMEM)
VMEM = pl.BlockSpec(memory_space=pltpu.VMEM)


def parameters(*semantics):
    return pltpu.CompilerParams(dimension_semantics=semantics or None, vmem_limit_bytes=VMEM_BYTES)


def forward_call(highest, bands, pair_ids, trims, weights, waves, points):
    length, fields = points.shape
    width = waves.shape[1]
    blocks = -(-length // BLOCK)
    return pl.pallas_call(
        functools.partial(forward_kernel, highest, bands),
        in_specs=[SMEM, SMEM, SMEM, VMEM, VMEM],
        out_specs=VMEM,
        out_shape=jax.ShapeDtypeStruct((4 * fields // LANES, width, LANES), jnp.bfloat16),
        scratch_shapes=[
            pltpu.VMEM((2 * width, blocks * BLOCK), jnp.bfloat16),
            pltpu.VMEM((2, 2 * width, fields), jnp.float32),
            pltpu.VMEM((width, LANES), jnp.float32),
            pltpu.VMEM((width, LANES), jnp.float32),
        ],
        compiler_params=parameters(),
        cost_estimate=pl.CostEstimate(
            flops=2 * length * fields * 2 * width, bytes_accessed=length * fields * 2, transcendentals=0
        ),
        name="forward_dft",
    )(pair_ids, trims, weights, waves, points)


def table_call(highest, length, pair_ids, trims, chunk_waves):
    blocks = -(-length // BLOCK)
    total = 2 * sum(waves.shape[1] for waves in chunk_waves)
    return pl.pallas_call(
        functools.partial(table_kernel, length, highest),
        in_specs=[SMEM, SMEM] + [VMEM] * len(chunk_waves),
        out_specs=VMEM,
        out_shape=jax.ShapeDtypeStruct((blocks * BLOCK, total), jnp.bfloat16),
        compiler_params=parameters(),
        cost_estimate=pl.CostEstimate(flops=8 * length * total, bytes_accessed=2 * length * total, transcendentals=0),
        name="inverse_table",
    )(pair_ids, trims, *chunk_waves)


def legendre_call(highest, start, band, wavenumbers, values, gathered, damping, spectrum):
    groups, local_pairs, degrees, each = gathered.shape
    count, cycles, _ = values.shape
    fields = LANES // 2
    previous = [] if spectrum is None else [spectrum]
    return pl.pallas_call(
        functools.partial(legendre_kernel, start, highest),
        grid=(count,),
        in_specs=[
            SMEM,
            SMEM,
            pl.BlockSpec((1, cycles, LANES), lambda q: (q, 0, 0)),
            pl.BlockSpec((groups, 1, degrees, each), lambda q: (0, q + start, 0, 0)),
            pl.BlockSpec(damping.shape, lambda q: (0, 0)),
        ]
        + [pl.BlockSpec(memory_space=pl.ANY)] * len(previous),
        out_specs=[
            pl.BlockSpec((1, fields, degrees), lambda q: (q + start, 0, 0)),
            pl.BlockSpec((1, cycles, LANES), lambda q: (q, 0, 0)),
        ],
        out_shape=[
            jax.ShapeDtypeStruct((local_pairs, fields, degrees), jnp.bfloat16),
            jax.ShapeDtypeStruct((count, cycles, LANES), jnp.bfloat16),
        ],
        input_output_aliases={5: 0} if previous else {},
        compiler_params=parameters("arbitrary"),
        cost_estimate=pl.CostEstimate(
            flops=4 * count * cycles * LANES * degrees,
            bytes_accessed=2 * count * cycles * degrees,
            transcendentals=0,
        ),
        name="legendre_both_ways",
    )(band, wavenumbers, values, gathered, damping, *previous)


def inverse_call(length, fields, pair_ids, values, table):
    blocks = -(-length // BLOCK)
    total = table.shape[1]
    return pl.pallas_call(
        functools.partial(inverse_kernel, len(values)),
        grid=(blocks,),
        in_specs=[SMEM]
        + [pl.BlockSpec(one.shape, lambda i: (0, 0, 0)) for one in values]
        + [pl.BlockSpec((BLOCK, total), lambda i: (i, 0))],
        out_specs=pl.BlockSpec((BLOCK, fields), lambda i: (i, 0)),
        out_shape=jax.ShapeDtypeStruct((length, fields), jnp.bfloat16),
        scratch_shapes=[
            pltpu.VMEM((4, max(one.shape[1] for one in values), LANES), jnp.float32),
            pltpu.VMEM((2, total, fields), jnp.bfloat16),
        ],
        compiler_params=parameters("arbitrary"),
        cost_estimate=pl.CostEstimate(
            flops=2 * length * fields * total, bytes_accessed=2 * length * (fields + total), transcendentals=0
        ),
        name="inverse_dft",
    )(pair_ids, *values, table)


def on_device(grid, pair_ids, trims, weights, wavenumbers, legendre, damping):
    fields, length = grid.shape[2:]
    columns = wavenumbers.shape[0]
    highest = columns - 1
    local_pairs, local_cycles, degrees = legendre.shape
    groups = lax.axis_size("fld")
    bands = lax.axis_size("band")
    gathered = lax.all_gather(legendre.swapaxes(1, 2), "fld")
    points = grid[0, 0].T
    by_band = wavenumbers.reshape(bands, local_pairs, 2)
    chunk_waves = [
        by_band[:, start:end].transpose(2, 0, 1).reshape(1, 2 * bands * (end - start)) for start, end in CHUNKS
    ]
    padding = -(-degrees // LANES) * LANES - columns
    padded = jnp.broadcast_to(jnp.pad(damping, (0, padding))[None, :], (8, columns + padding))
    band = (lax.axis_index("band") * local_pairs).astype(jnp.int32).reshape(1)

    arrived = []
    for (start, end), waves in zip(CHUNKS, chunk_waves):
        packed = forward_call(highest, bands, pair_ids, trims, weights, waves, points)
        packed = packed.reshape(groups * bands, end - start, 2, LANES)
        arrived.append(lax.all_to_all(packed, ("fld", "band"), split_axis=0, concat_axis=0, tiled=True))
    table = table_call(highest, length, pair_ids, trims, chunk_waves)
    spectrum = None
    returned = []
    for (start, end), message in zip(CHUNKS, arrived):
        values = message.transpose(1, 0, 2, 3).reshape(end - start, groups * local_cycles, LANES)
        spectrum, rebuilt = legendre_call(
            highest, start, band, wavenumbers, values, gathered, padded, spectrum
        )
        leaving = rebuilt.reshape(end - start, groups * bands, 2, LANES).transpose(1, 0, 2, 3)
        message = lax.all_to_all(leaving, ("fld", "band"), split_axis=0, concat_axis=0, tiled=True)
        returned.append(message.reshape(groups, bands * (end - start) * 2, LANES))
    restored = inverse_call(length, fields, pair_ids, returned, table)
    return (
        spectrum.reshape(local_pairs, 2, fields // groups, degrees),
        restored.T.reshape(1, 1, fields, length),
    )


def solution(mesh):
    placed = (
        P("fld", "band", None, None),
        P("fld", "band"),
        P("fld", "band", None),
        P("fld", "band", None),
        P(),
        P("band", "fld", None),
        P(),
    )
    return jax.shard_map(
        on_device,
        mesh=mesh,
        in_specs=placed,
        out_specs=(P("band", None, "fld", None), P("fld", "band", None, None)),
        check_vma=False,
    )
```

```python
import functools

import jax
import jax.numpy as jnp
import numpy as np
from jax import lax
from jax.experimental import pallas as pl
from jax.experimental.pallas import tpu as pltpu
from jax.sharding import PartitionSpec as P

PI = 3.141592653589793
LANES = 128
STEP = 512
INVERSE_BLOCK = 656
STRIP = 64
VMEM_BYTES = 56 * 1024 * 1024
CHUNKS = ((0, 5),)
RING = 8
BAND_ORDER = [
    RING * sum((p >> (5 - 2 * bit) & 1) << bit for bit in range(3)) + sum((p >> (4 - 2 * bit) & 1) << bit for bit in range(3))
    for p in range(RING * RING)
]


def unit_circle(waves, points, count):
    inverse = 1.0 / count
    product = waves * points
    residue = product - jnp.round(product * inverse) * count
    half = residue * (inverse * PI)
    square = half * half
    sine = 1.0 / 6227020800.0
    for term in (-1.0 / 39916800.0, 1.0 / 362880.0, -1.0 / 5040.0, 1.0 / 120.0, -1.0 / 6.0, 1.0):
        sine = sine * square + term
    sine = sine * half
    cosine = 1.0 / 479001600.0
    for term in (-1.0 / 3628800.0, 1.0 / 40320.0, -1.0 / 720.0, 1.0 / 24.0, -0.5, 1.0):
        cosine = cosine * square + term
    return cosine * cosine - sine * sine, -2.0 * sine * cosine


def turn(state, step):
    cosine, sine = state
    return cosine * step[0] - sine * step[1], sine * step[0] + cosine * step[1]


def cycle_facts(length, highest, pair_ids, trims):
    first = 20 + 4 * pair_ids[0, 0]
    counts = (first, length - first)
    limits = [
        jnp.maximum(jnp.minimum(highest, count // 2 - 1) - trims[0, 0, cycle], 0)
        for cycle, count in enumerate(counts)
    ]
    return first, [c.astype(jnp.float32) for c in counts], [l.astype(jnp.float32) for l in limits]


def fill_table(axis, chosen, step_waves, facts, blocks, write):
    first, counts, limits = facts
    shape = chosen.shape
    lane = lax.broadcasted_iota(jnp.int32, shape, axis)
    straddle = first // LANES

    def begin(cycle, offset):
        state = unit_circle(chosen, (lane + offset).astype(jnp.float32), counts[cycle])
        kept = chosen <= limits[cycle]
        return tuple(jnp.where(kept, part, 0.0) for part in state)

    steps = step_waves(counts)

    def advance(cycle):
        def body(block, state):
            write(block, state)
            return turn(state, steps[cycle])

        return body

    state = lax.fori_loop(0, straddle, advance(0), begin(0, 0))
    offset = straddle * LANES - first
    later = begin(1, offset)
    before = lane + offset < 0
    write(straddle, tuple(jnp.where(before, old, new) for old, new in zip(state, later)))
    lax.fori_loop(straddle + 1, blocks, advance(1), turn(later, steps[1]))


def ordered_columns(chunk, wavenumbers, raw, columns):
    total = wavenumbers.shape[1]
    stride = total // len(BAND_ORDER)
    count = chunk[1] - chunk[0]
    raw[...] = jnp.broadcast_to(wavenumbers[...].astype(jnp.float32), (LANES, total)).T
    for column in range(2):
        for place, band in enumerate(BAND_ORDER):
            target = (column * len(BAND_ORDER) + place) * count
            columns[target:target + count, :] = raw[pl.ds(band * stride + 2 * chunk[0] + column, count, stride=2), :]


def forward_kernel(highest, chunk, pair_ids, trims, weights, wavenumbers, grid, packed, table, totals, raw, columns, rows):
    length, fields = grid.shape
    width = columns.shape[0]
    quarter = width // 2
    facts = cycle_facts(length, highest, pair_ids, trims)
    first, counts, _ = facts
    blocks = -(-length // LANES)
    ordered_columns(chunk, wavenumbers, raw, columns)

    for strip in range(width // STRIP):
        chosen = columns[strip * STRIP:(strip + 1) * STRIP, :]

        def step_waves(counts):
            cycle_lane = lax.broadcasted_iota(jnp.int32, chosen.shape, 1)
            count = jnp.where(cycle_lane == 0, counts[0], counts[1])
            cosine, sine = unit_circle(chosen, float(LANES), count)
            return [
                tuple(jnp.broadcast_to(part[:, c:c + 1], chosen.shape) for part in (cosine, sine))
                for c in range(2)
            ]

        def write(block, state):
            for part in range(2):
                table[
                    part * width + strip * STRIP:part * width + (strip + 1) * STRIP,
                    pl.ds(pl.multiple_of(block * LANES, LANES), LANES),
                ] = state[part].astype(jnp.bfloat16)

        fill_table(1, chosen, step_waves, facts, blocks, write)

    full = length // STEP
    straddle = first // STEP
    position = lax.broadcasted_iota(jnp.int32, (STEP, fields), 0)

    def product(start, size, data):
        return jnp.dot(table[:, pl.ds(start, size)], data, preferred_element_type=jnp.float32)

    def data_of(block):
        return grid[pl.ds(pl.multiple_of(block * STEP, STEP), STEP), :]

    def add(cycle):
        def body(block, carry):
            totals[cycle] += product(pl.multiple_of(block * STEP, STEP), STEP, data_of(block))
            return carry

        return body

    data = data_of(straddle)
    before = position + straddle * STEP < first
    nothing = jnp.zeros_like(data)
    start = pl.multiple_of(straddle * STEP, STEP)
    totals[0] = product(start, STEP, jnp.where(before, data, nothing))
    totals[1] = product(start, STEP, jnp.where(before, nothing, data))
    lax.fori_loop(0, straddle, add(0), 0)
    lax.fori_loop(straddle + 1, full, add(1), 0)
    totals[1] += product(full * STEP, length - full * STEP, grid[full * STEP:, :])

    share = LANES // 4
    for group in range(fields // share):
        lanes = slice(group * share, (group + 1) * share)
        for cycle in range(2):
            scale = jnp.full((1, LANES), weights[0, 0, cycle]) / counts[cycle]
            joined = jnp.concatenate(
                [totals[cycle, part * quarter:(part + 1) * quarter, lanes] for part in (0, 2, 1, 3)], axis=1
            )
            rows[pl.ds(cycle, quarter, stride=2), :] = joined * scale
        packed[group] = rows[...].astype(jnp.bfloat16)


def table_kernel(length, highest, pair_ids, trims, wavenumbers, table, raw, columns):
    facts = cycle_facts(length, highest, pair_ids, trims)
    blocks = -(-length // LANES)
    base = 0
    for chunk in CHUNKS:
        width = 2 * len(BAND_ORDER) * (chunk[1] - chunk[0])
        ordered_columns(chunk, wavenumbers, raw, columns)
        for tile in range(width // LANES):
            chosen = columns[tile * LANES:(tile + 1) * LANES, :].T

            def step_waves(counts):
                return [
                    tuple(part[:1] for part in unit_circle(chosen[:8], float(LANES), count)) for count in counts
                ]

            def write(block, state):
                for part in range(2):
                    left = base + part * width + tile * LANES
                    table[pl.ds(pl.multiple_of(block * LANES, LANES), LANES), left:left + LANES] = (
                        state[part].astype(jnp.bfloat16)
                    )

            fill_table(0, chosen, step_waves, facts, blocks, write)
        base += 2 * width


def legendre_kernel(start, highest, band, wavenumbers, ordering, values, legendre, damping, *refs):
    spectrum, rebuilt = refs[-2:]
    groups, _, degrees, each = legendre.shape
    matrix = jnp.concatenate([legendre[group, 0] for group in range(groups)], axis=1)
    from_order = ordering[...].T
    natural = [
        jnp.dot(from_order, values[0, group * each:(group + 1) * each], preferred_element_type=jnp.float32)
        for group in range(groups)
    ]
    natural = jnp.concatenate(natural, axis=0).astype(jnp.bfloat16)
    sums = jnp.dot(matrix, natural, preferred_element_type=jnp.float32).T
    fields = sums.shape[0] // 2
    pair = band[0] + start + pl.program_id(0)
    first_wave = wavenumbers[2 * pair]
    second_wave = wavenumbers[2 * pair + 1]
    width = damping.shape[1]
    degree = lax.broadcasted_iota(jnp.int32, (1, width), 1)
    kept = degree < highest + 1 - first_wave
    upper = pltpu.roll(damping[...], lax.rem(width - first_wave, width), 1)
    lower = pltpu.roll(damping[...], 1, 1)
    factor = jnp.where(kept, upper[:1], lower[:1])[:, :degrees]
    head = jnp.broadcast_to(kept[:, :degrees], (fields, degrees))
    filtered = (jnp.where(head, sums[:fields], sums[fields:]) * factor).astype(jnp.bfloat16)
    spectrum[0] = filtered
    nothing = jnp.zeros_like(filtered)
    parts = jnp.concatenate([jnp.where(head, filtered, nothing), jnp.where(head, nothing, filtered)], axis=0)
    products = jnp.dot(parts, matrix, preferred_element_type=jnp.float32)
    row = lax.broadcasted_iota(jnp.int32, products.shape, 0)
    wave = jnp.where(row < fields, first_wave, second_wave)
    doubled = products * jnp.where(wave == 0, 1.0, 2.0)
    doubled = doubled.astype(jnp.bfloat16)
    for group in range(groups):
        part = slice(group * each, (group + 1) * each)
        rebuilt[0, part] = lax.dot_general(
            ordering[...], doubled[:, part], (((1,), (1,)), ((), ())), preferred_element_type=jnp.float32
        ).astype(jnp.bfloat16)


def inverse_kernel(chunks, pair_ids, *refs):
    values = refs[:chunks]
    table, restored, rows, factors = refs[chunks:]
    block = pl.program_id(0)
    first = 20 + 4 * pair_ids[0, 0]
    share = LANES // 4

    @pl.when(block == 0)
    def _():
        base = 0
        for chunk in values:
            groups, height, _ = chunk.shape
            quarter = height // 2
            for side in range(groups // 4):
                for near in range(4):
                    rows[near, :height] = chunk[4 * side + near].astype(jnp.float32)
                for cycle in range(2):
                    turned = [
                        rows[near, pl.ds(cycle, quarter, stride=2), :].astype(jnp.bfloat16) for near in range(4)
                    ]
                    for part in range(4):
                        source = (0, 2, 1, 3)[part] * share
                        factors[
                            cycle,
                            base + part * quarter:base + (part + 1) * quarter,
                            side * LANES:(side + 1) * LANES,
                        ] = jnp.concatenate([one[:, source:source + share] for one in turned], axis=1)
            base += 4 * quarter

    def product(cycle):
        return jnp.dot(table[...], factors[cycle], preferred_element_type=jnp.float32)

    start = block * INVERSE_BLOCK
    end = start + INVERSE_BLOCK

    @pl.when(end <= first)
    def _():
        restored[...] = product(0).astype(jnp.bfloat16)

    @pl.when(start >= first)
    def _():
        restored[...] = product(1).astype(jnp.bfloat16)

    @pl.when((start < first) & (end > first))
    def _():
        position = start + lax.broadcasted_iota(jnp.int32, restored.shape, 0)
        restored[...] = jnp.where(position < first, product(0), product(1)).astype(jnp.bfloat16)


SMEM = pl.BlockSpec(memory_space=pltpu.SMEM)
VMEM = pl.BlockSpec(memory_space=pltpu.VMEM)


def parameters(*semantics):
    return pltpu.CompilerParams(dimension_semantics=semantics or None, vmem_limit_bytes=VMEM_BYTES)


def forward_call(highest, chunk, pair_ids, trims, weights, wavenumbers, points):
    length, fields = points.shape
    width = 2 * len(BAND_ORDER) * (chunk[1] - chunk[0])
    blocks = -(-length // LANES)
    return pl.pallas_call(
        functools.partial(forward_kernel, highest, chunk),
        in_specs=[SMEM, SMEM, SMEM, VMEM, VMEM],
        out_specs=VMEM,
        out_shape=jax.ShapeDtypeStruct((4 * fields // LANES, width, LANES), jnp.bfloat16),
        scratch_shapes=[
            pltpu.VMEM((2 * width, blocks * LANES), jnp.bfloat16),
            pltpu.VMEM((2, 2 * width, fields), jnp.float32),
            pltpu.VMEM((wavenumbers.shape[1], LANES), jnp.float32),
            pltpu.VMEM((width, LANES), jnp.float32),
            pltpu.VMEM((width, LANES), jnp.float32),
        ],
        compiler_params=parameters(),
        cost_estimate=pl.CostEstimate(
            flops=2 * length * fields * 2 * width, bytes_accessed=length * fields * 2, transcendentals=0
        ),
        name="forward_dft",
    )(pair_ids, trims, weights, wavenumbers, points)


def table_call(highest, length, pair_ids, trims, wavenumbers):
    blocks = -(-length // LANES)
    total = 2 * wavenumbers.shape[1]
    return pl.pallas_call(
        functools.partial(table_kernel, length, highest),
        in_specs=[SMEM, SMEM, VMEM],
        out_specs=VMEM,
        out_shape=jax.ShapeDtypeStruct((blocks * LANES, total), jnp.bfloat16),
        scratch_shapes=[
            pltpu.VMEM((wavenumbers.shape[1], LANES), jnp.float32),
            pltpu.VMEM((wavenumbers.shape[1], LANES), jnp.float32),
        ],
        compiler_params=parameters(),
        cost_estimate=pl.CostEstimate(flops=8 * length * total, bytes_accessed=2 * length * total, transcendentals=0),
        name="inverse_table",
    )(pair_ids, trims, wavenumbers)


def legendre_call(highest, start, band, wavenumbers, values, gathered, damping, spectrum):
    groups, local_pairs, degrees, each = gathered.shape
    count, cycles, _ = values.shape
    fields = LANES // 2
    previous = [] if spectrum is None else [spectrum]
    ordering = np.zeros((len(BAND_ORDER), 2, len(BAND_ORDER), 2), np.float32)
    for place, one in enumerate(BAND_ORDER):
        ordering[place, 0, one, 0] = ordering[place, 1, one, 1] = 1.0
    ordering = jnp.asarray(ordering.reshape(each, each), jnp.bfloat16)
    return pl.pallas_call(
        functools.partial(legendre_kernel, start, highest),
        grid=(count,),
        in_specs=[
            SMEM,
            SMEM,
            pl.BlockSpec(ordering.shape, lambda q: (0, 0)),
            pl.BlockSpec((1, cycles, LANES), lambda q: (q, 0, 0)),
            pl.BlockSpec((groups, 1, degrees, each), lambda q: (0, q + start, 0, 0)),
            pl.BlockSpec(damping.shape, lambda q: (0, 0)),
        ]
        + [pl.BlockSpec(memory_space=pl.ANY)] * len(previous),
        out_specs=[
            pl.BlockSpec((1, fields, degrees), lambda q: (q + start, 0, 0)),
            pl.BlockSpec((1, cycles, LANES), lambda q: (q, 0, 0)),
        ],
        out_shape=[
            jax.ShapeDtypeStruct((local_pairs, fields, degrees), jnp.bfloat16),
            jax.ShapeDtypeStruct((count, cycles, LANES), jnp.bfloat16),
        ],
        input_output_aliases={6: 0} if previous else {},
        compiler_params=parameters("arbitrary"),
        cost_estimate=pl.CostEstimate(
            flops=4 * count * cycles * LANES * degrees,
            bytes_accessed=2 * count * cycles * degrees,
            transcendentals=0,
        ),
        name="legendre_both_ways",
    )(band, wavenumbers, ordering, values, gathered, damping, *previous)


def inverse_call(length, fields, pair_ids, values, table):
    blocks = -(-length // INVERSE_BLOCK)
    total = table.shape[1]
    return pl.pallas_call(
        functools.partial(inverse_kernel, len(values)),
        grid=(blocks,),
        in_specs=[SMEM]
        + [pl.BlockSpec(one.shape, lambda i: (0, 0, 0)) for one in values]
        + [pl.BlockSpec((INVERSE_BLOCK, total), lambda i: (i, 0))],
        out_specs=pl.BlockSpec((INVERSE_BLOCK, fields), lambda i: (i, 0)),
        out_shape=jax.ShapeDtypeStruct((length, fields), jnp.bfloat16),
        scratch_shapes=[
            pltpu.VMEM((4, max(one.shape[1] for one in values), LANES), jnp.float32),
            pltpu.VMEM((2, total, fields), jnp.bfloat16),
        ],
        compiler_params=parameters("arbitrary"),
        cost_estimate=pl.CostEstimate(
            flops=2 * length * fields * total, bytes_accessed=2 * length * (fields + total), transcendentals=0
        ),
        name="inverse_dft",
    )(pair_ids, *values, table)


def exchange(message, groups):
    bands = len(BAND_ORDER)
    partners = [group * bands + band for group in range(groups) for band in BAND_ORDER]
    return lax.all_to_all(
        message, ("fld", "band"), split_axis=0, concat_axis=0, tiled=True, axis_index_groups=[partners]
    )


def on_device(grid, pair_ids, trims, weights, wavenumbers, legendre, damping):
    fields, length = grid.shape[2:]
    columns = wavenumbers.shape[0]
    highest = columns - 1
    local_pairs, local_cycles, degrees = legendre.shape
    groups = lax.axis_size("fld")
    bands = lax.axis_size("band")
    gathered = lax.all_gather(legendre.swapaxes(1, 2), "fld")
    points = grid[0, 0].T
    waves = wavenumbers[None, :]
    padding = -(-degrees // LANES) * LANES - columns
    padded = jnp.broadcast_to(jnp.pad(damping, (0, padding))[None, :], (8, columns + padding))
    band = (lax.axis_index("band") * local_pairs).astype(jnp.int32).reshape(1)

    arrived = []
    for chunk in CHUNKS:
        packed = forward_call(highest, chunk, pair_ids, trims, weights, waves, points)
        arrived.append(exchange(packed.reshape(groups * bands, chunk[1] - chunk[0], 2, LANES), groups))
    table = table_call(highest, length, pair_ids, trims, waves)
    spectrum = None
    returned = []
    for (start, end), message in zip(CHUNKS, arrived):
        count = end - start
        values = message.transpose(1, 0, 2, 3).reshape(count, groups * local_cycles, LANES)
        spectrum, rebuilt = legendre_call(
            highest, start, band, wavenumbers, values, gathered, padded, spectrum
        )
        leaving = rebuilt.reshape(count, groups * bands, 2, LANES).transpose(1, 0, 2, 3)
        message = exchange(leaving, groups)
        returned.append(message.reshape(groups, bands * count * 2, LANES))
    restored = inverse_call(length, fields, pair_ids, returned, table)
    return (
        spectrum.reshape(local_pairs, 2, fields // groups, degrees),
        restored.T.reshape(1, 1, fields, length),
    )


def solution(mesh):
    placed = (
        P("fld", "band", None, None),
        P("fld", "band"),
        P("fld", "band", None),
        P("fld", "band", None),
        P(),
        P("band", "fld", None),
        P(),
    )
    return jax.shard_map(
        on_device,
        mesh=mesh,
        in_specs=placed,
        out_specs=(P("band", None, "fld", None), P("fld", "band", None, None)),
        check_vma=False,
    )
```

```python
import functools

import jax
import jax.numpy as jnp
from jax import lax
from jax.experimental import pallas as pl
from jax.experimental.pallas import tpu as pltpu
from jax.sharding import PartitionSpec as P

PI = 3.141592653589793
LANES = 128
STEP = 512
INVERSE_BLOCK = 656
STRIP = 64
VMEM_BYTES = 40 * 1024 * 1024
LARGE_VMEM_BYTES = 57_000_000
CHUNKS = ((0, 3), (3, 5))


def unit_circle(waves, points, count):
    inverse = 1.0 / count
    product = waves * points
    residue = product - jnp.round(product * inverse) * count
    half = residue * (inverse * PI)
    square = half * half
    sine = 1.0 / 6227020800.0
    for term in (-1.0 / 39916800.0, 1.0 / 362880.0, -1.0 / 5040.0, 1.0 / 120.0, -1.0 / 6.0, 1.0):
        sine = sine * square + term
    sine = sine * half
    cosine = 1.0 / 479001600.0
    for term in (-1.0 / 3628800.0, 1.0 / 40320.0, -1.0 / 720.0, 1.0 / 24.0, -0.5, 1.0):
        cosine = cosine * square + term
    return cosine * cosine - sine * sine, -2.0 * sine * cosine


def turn(state, step):
    cosine, sine = state
    return cosine * step[0] - sine * step[1], sine * step[0] + cosine * step[1]


def cycle_facts(length, highest, pair_ids, trims):
    first = 20 + 4 * pair_ids[0, 0]
    counts = (first, length - first)
    limits = [
        jnp.maximum(jnp.minimum(highest, count // 2 - 1) - trims[0, 0, cycle], 0)
        for cycle, count in enumerate(counts)
    ]
    return first, [c.astype(jnp.float32) for c in counts], [l.astype(jnp.float32) for l in limits]


def fill_table(axis, chosen, step_waves, facts, blocks, write):
    first, counts, limits = facts
    shape = chosen.shape
    lane = lax.broadcasted_iota(jnp.int32, shape, axis)
    straddle = first // LANES

    def begin(cycle, offset):
        state = unit_circle(chosen, (lane + offset).astype(jnp.float32), counts[cycle])
        kept = chosen <= limits[cycle]
        return tuple(jnp.where(kept, part, 0.0) for part in state)

    steps = step_waves(counts)

    def advance(cycle):
        def body(block, state):
            write(block, state)
            return turn(state, steps[cycle])

        return body

    state = lax.fori_loop(0, straddle, advance(0), begin(0, 0))
    offset = straddle * LANES - first
    later = begin(1, offset)
    before = lane + offset < 0
    write(straddle, tuple(jnp.where(before, old, new) for old, new in zip(state, later)))
    lax.fori_loop(straddle + 1, blocks, advance(1), turn(later, steps[1]))


def ordered_columns(chunk, stride, wavenumbers, raw, columns):
    total = wavenumbers.shape[0]
    raw[...] = jnp.broadcast_to(wavenumbers[...].astype(jnp.float32)[None, :], (LANES, total)).T
    target = 0
    for column in range(2):
        for pair in range(*chunk):
            columns[target:target + STRIP, :] = raw[pl.ds(2 * pair + column, STRIP, stride=stride), :]
            target += STRIP


def forward_kernel(highest, chunk, stride, pair_ids, trims, weights, wavenumbers, grid, packed, table, totals, raw, columns, rows):
    length, fields = grid.shape
    width = columns.shape[0]
    quarter = width // 2
    facts = cycle_facts(length, highest, pair_ids, trims)
    first, counts, _ = facts
    blocks = -(-length // LANES)
    ordered_columns(chunk, stride, wavenumbers, raw, columns)

    for strip in range(width // STRIP):
        chosen = columns[strip * STRIP:(strip + 1) * STRIP, :]

        def step_waves(counts):
            cycle_lane = lax.broadcasted_iota(jnp.int32, chosen.shape, 1)
            count = jnp.where(cycle_lane == 0, counts[0], counts[1])
            cosine, sine = unit_circle(chosen, float(LANES), count)
            return [
                tuple(jnp.broadcast_to(part[:, c:c + 1], chosen.shape) for part in (cosine, sine))
                for c in range(2)
            ]

        def write(block, state):
            for part in range(2):
                table[
                    part * width + strip * STRIP:part * width + (strip + 1) * STRIP,
                    pl.ds(pl.multiple_of(block * LANES, LANES), LANES),
                ] = state[part].astype(jnp.bfloat16)

        fill_table(1, chosen, step_waves, facts, blocks, write)

    full = length // STEP
    straddle = first // STEP
    position = lax.broadcasted_iota(jnp.int32, (STEP, fields), 0)

    def product(start, size, data):
        return jnp.dot(table[:, pl.ds(start, size)], data, preferred_element_type=jnp.float32)

    def data_of(block):
        return grid[pl.ds(pl.multiple_of(block * STEP, STEP), STEP), :]

    def add(cycle):
        def body(block, carry):
            totals[cycle] += product(pl.multiple_of(block * STEP, STEP), STEP, data_of(block))
            return carry

        return body

    data = data_of(straddle)
    before = position + straddle * STEP < first
    nothing = jnp.zeros_like(data)
    start = pl.multiple_of(straddle * STEP, STEP)
    totals[0] = product(start, STEP, jnp.where(before, data, nothing))
    totals[1] = product(start, STEP, jnp.where(before, nothing, data))
    lax.fori_loop(0, straddle, add(0), 0)
    lax.fori_loop(straddle + 1, full, add(1), 0)
    totals[1] += product(full * STEP, length - full * STEP, grid[full * STEP:, :])

    share = LANES // 4
    for group in range(fields // share):
        lanes = slice(group * share, (group + 1) * share)
        for cycle in range(2):
            scale = jnp.full((1, LANES), weights[0, 0, cycle]) / counts[cycle]
            joined = jnp.concatenate(
                [totals[cycle, part * quarter:(part + 1) * quarter, lanes] for part in (0, 2, 1, 3)], axis=1
            )
            joined = joined * scale
            for pair in range(quarter // STRIP):
                rows[pl.ds(2 * pair + cycle, STRIP, stride=2 * quarter // STRIP), :] = (
                    joined[pair * STRIP:(pair + 1) * STRIP]
                )
        packed[group] = rows[...].astype(jnp.bfloat16)


def table_kernel(length, highest, stride, pair_ids, trims, wavenumbers, table, raw, columns):
    facts = cycle_facts(length, highest, pair_ids, trims)
    blocks = -(-length // LANES)
    base = 0
    for chunk in CHUNKS:
        width = 2 * STRIP * (chunk[1] - chunk[0])
        ordered_columns(chunk, stride, wavenumbers, raw, columns)
        for tile in range(width // LANES):
            chosen = columns[tile * LANES:(tile + 1) * LANES, :].T

            def step_waves(counts):
                return [
                    tuple(part[:1] for part in unit_circle(chosen[:8], float(LANES), count)) for count in counts
                ]

            def write(block, state):
                for part in range(2):
                    left = base + part * width + tile * LANES
                    table[pl.ds(pl.multiple_of(block * LANES, LANES), LANES), left:left + LANES] = (
                        state[part].astype(jnp.bfloat16)
                    )

            fill_table(0, chosen, step_waves, facts, blocks, write)
        base += 2 * width


def legendre_kernel(start, highest, band, wavenumbers, values, legendre, damping, *refs):
    spectrum, rebuilt = refs[-2:]
    groups, _, degrees, each = legendre.shape
    matrix = jnp.concatenate([legendre[group, 0] for group in range(groups)], axis=1)
    sums = lax.dot_general(
        values[0].T, matrix, (((1,), (1,)), ((), ())), preferred_element_type=jnp.float32
    )
    fields = sums.shape[0] // 2
    pair = band[0] + start + pl.program_id(0)
    first_wave = wavenumbers[2 * pair]
    second_wave = wavenumbers[2 * pair + 1]
    width = damping.shape[1]
    degree = lax.broadcasted_iota(jnp.int32, (1, width), 1)
    kept = degree < highest + 1 - first_wave
    upper = pltpu.roll(damping[...], lax.rem(width - first_wave, width), 1)
    lower = pltpu.roll(damping[...], 1, 1)
    factor = jnp.where(kept, upper[:1], lower[:1])[:, :degrees]
    head = jnp.broadcast_to(kept[:, :degrees], (fields, degrees))
    filtered = (jnp.where(head, sums[:fields], sums[fields:]) * factor).astype(jnp.bfloat16)
    spectrum[0] = filtered
    nothing = jnp.zeros_like(filtered)
    parts = jnp.concatenate([jnp.where(head, filtered, nothing), jnp.where(head, nothing, filtered)], axis=0)
    products = jnp.dot(parts, matrix, preferred_element_type=jnp.float32)
    row = lax.broadcasted_iota(jnp.int32, products.shape, 0)
    wave = jnp.where(row < fields, first_wave, second_wave)
    doubled = products * jnp.where(wave == 0, 1.0, 2.0)
    rebuilt[0] = doubled.astype(jnp.bfloat16).T


def inverse_kernel(chunks, pair_ids, *refs):
    values = refs[:chunks]
    table, restored, rows, factors = refs[chunks:]
    block = pl.program_id(0)
    first = 20 + 4 * pair_ids[0, 0]
    share = LANES // 4

    @pl.when(block == 0)
    def _():
        base = 0
        for chunk in values:
            groups, height, _ = chunk.shape
            quarter = height // 2
            for side in range(groups // 4):
                for near in range(4):
                    rows[near, :height] = chunk[4 * side + near].astype(jnp.float32)
                for cycle in range(2):
                    turned = [
                        jnp.concatenate(
                            [
                                rows[near, pl.ds(2 * pair + cycle, STRIP, stride=2 * quarter // STRIP), :]
                                for pair in range(quarter // STRIP)
                            ],
                            axis=0,
                        ).astype(jnp.bfloat16)
                        for near in range(4)
                    ]
                    for part in range(4):
                        source = (0, 2, 1, 3)[part] * share
                        factors[
                            cycle,
                            base + part * quarter:base + (part + 1) * quarter,
                            side * LANES:(side + 1) * LANES,
                        ] = jnp.concatenate([one[:, source:source + share] for one in turned], axis=1)
            base += 4 * quarter

    def product(cycle):
        return jnp.dot(table[...], factors[cycle], preferred_element_type=jnp.float32)

    start = block * INVERSE_BLOCK
    end = start + INVERSE_BLOCK

    @pl.when(end <= first)
    def _():
        restored[...] = product(0).astype(jnp.bfloat16)

    @pl.when(start >= first)
    def _():
        restored[...] = product(1).astype(jnp.bfloat16)

    @pl.when((start < first) & (end > first))
    def _():
        position = start + lax.broadcasted_iota(jnp.int32, restored.shape, 0)
        restored[...] = jnp.where(position < first, product(0), product(1)).astype(jnp.bfloat16)


SMEM = pl.BlockSpec(memory_space=pltpu.SMEM)
VMEM = pl.BlockSpec(memory_space=pltpu.VMEM)


def parameters(*semantics, limit=VMEM_BYTES):
    return pltpu.CompilerParams(dimension_semantics=semantics or None, vmem_limit_bytes=limit)


def forward_call(highest, chunk, stride, pair_ids, trims, weights, wavenumbers, points):
    length, fields = points.shape
    width = 2 * STRIP * (chunk[1] - chunk[0])
    blocks = -(-length // LANES)
    return pl.pallas_call(
        functools.partial(forward_kernel, highest, chunk, stride),
        in_specs=[SMEM, SMEM, SMEM, VMEM, VMEM],
        out_specs=VMEM,
        out_shape=jax.ShapeDtypeStruct((4 * fields // LANES, width, LANES), jnp.bfloat16),
        scratch_shapes=[
            pltpu.VMEM((2 * width, blocks * LANES), jnp.bfloat16),
            pltpu.VMEM((2, 2 * width, fields), jnp.float32),
            pltpu.VMEM((wavenumbers.shape[0], LANES), jnp.float32),
            pltpu.VMEM((width, LANES), jnp.float32),
            pltpu.VMEM((width, LANES), jnp.float32),
        ],
        compiler_params=parameters(),
        cost_estimate=pl.CostEstimate(
            flops=2 * length * fields * 2 * width, bytes_accessed=length * fields * 2, transcendentals=0
        ),
        name="forward_dft",
    )(pair_ids, trims, weights, wavenumbers, points)


def table_call(highest, length, stride, pair_ids, trims, wavenumbers):
    blocks = -(-length // LANES)
    total = 2 * wavenumbers.shape[0]
    return pl.pallas_call(
        functools.partial(table_kernel, length, highest, stride),
        in_specs=[SMEM, SMEM, VMEM],
        out_specs=VMEM,
        out_shape=jax.ShapeDtypeStruct((blocks * LANES, total), jnp.bfloat16),
        scratch_shapes=[
            pltpu.VMEM((wavenumbers.shape[0], LANES), jnp.float32),
            pltpu.VMEM((wavenumbers.shape[0], LANES), jnp.float32),
        ],
        compiler_params=parameters(),
        cost_estimate=pl.CostEstimate(flops=8 * length * total, bytes_accessed=2 * length * total, transcendentals=0),
        name="inverse_table",
    )(pair_ids, trims, wavenumbers)


def legendre_call(highest, start, band, wavenumbers, values, gathered, damping, spectrum):
    groups, local_pairs, degrees, each = gathered.shape
    count, cycles, _ = values.shape
    fields = LANES // 2
    previous = [] if spectrum is None else [spectrum]
    return pl.pallas_call(
        functools.partial(legendre_kernel, start, highest),
        grid=(count,),
        in_specs=[
            SMEM,
            SMEM,
            pl.BlockSpec((1, cycles, LANES), lambda q: (q, 0, 0)),
            pl.BlockSpec((groups, 1, degrees, each), lambda q: (0, q + start, 0, 0)),
            pl.BlockSpec(damping.shape, lambda q: (0, 0)),
        ]
        + [pl.BlockSpec(memory_space=pl.ANY)] * len(previous),
        out_specs=[
            pl.BlockSpec((1, fields, degrees), lambda q: (q + start, 0, 0)),
            pl.BlockSpec((1, cycles, LANES), lambda q: (q, 0, 0)),
        ],
        out_shape=[
            jax.ShapeDtypeStruct((local_pairs, fields, degrees), jnp.bfloat16),
            jax.ShapeDtypeStruct((count, cycles, LANES), jnp.bfloat16),
        ],
        input_output_aliases={5: 0} if previous else {},
        compiler_params=parameters("arbitrary", limit=LARGE_VMEM_BYTES),
        cost_estimate=pl.CostEstimate(
            flops=4 * count * cycles * LANES * degrees,
            bytes_accessed=2 * count * cycles * degrees,
            transcendentals=0,
        ),
        name="legendre_both_ways",
    )(band, wavenumbers, values, gathered, damping, *previous)


def inverse_call(length, fields, pair_ids, values, table):
    blocks = -(-length // INVERSE_BLOCK)
    total = table.shape[1]
    return pl.pallas_call(
        functools.partial(inverse_kernel, len(values)),
        grid=(blocks,),
        in_specs=[SMEM]
        + [pl.BlockSpec(one.shape, lambda i: (0, 0, 0)) for one in values]
        + [pl.BlockSpec((INVERSE_BLOCK, total), lambda i: (i, 0))],
        out_specs=pl.BlockSpec((INVERSE_BLOCK, fields), lambda i: (i, 0)),
        out_shape=jax.ShapeDtypeStruct((length, fields), jnp.bfloat16),
        scratch_shapes=[
            pltpu.VMEM((4, max(one.shape[1] for one in values), LANES), jnp.float32),
            pltpu.VMEM((2, total, fields), jnp.bfloat16),
        ],
        compiler_params=parameters("arbitrary", limit=LARGE_VMEM_BYTES),
        cost_estimate=pl.CostEstimate(
            flops=2 * length * fields * total, bytes_accessed=2 * length * (fields + total), transcendentals=0
        ),
        name="inverse_dft",
    )(pair_ids, *values, table)


def exchange(message):
    return lax.all_to_all(message, ("fld", "band"), split_axis=0, concat_axis=0, tiled=True)


def on_device(grid, pair_ids, trims, weights, wavenumbers, legendre, damping):
    fields, length = grid.shape[2:]
    columns = wavenumbers.shape[0]
    highest = columns - 1
    local_pairs, local_cycles, degrees = legendre.shape
    groups = lax.axis_size("fld")
    bands = lax.axis_size("band")
    gathered = lax.all_gather(legendre.swapaxes(1, 2), "fld")
    points = grid[0, 0].T
    stride = 2 * local_pairs
    padding = -(-degrees // LANES) * LANES - columns
    padded = jnp.broadcast_to(jnp.pad(damping, (0, padding))[None, :], (8, columns + padding))
    band = (lax.axis_index("band") * local_pairs).astype(jnp.int32).reshape(1)

    arrived = []
    for chunk in CHUNKS:
        packed = forward_call(highest, chunk, stride, pair_ids, trims, weights, wavenumbers, points)
        arrived.append(exchange(packed.reshape(groups * bands, chunk[1] - chunk[0], 2, LANES)))
    table = table_call(highest, length, stride, pair_ids, trims, wavenumbers)
    spectrum = None
    returned = []
    for (start, end), message in zip(CHUNKS, arrived):
        count = end - start
        values = message.transpose(1, 0, 2, 3).reshape(count, groups * local_cycles, LANES)
        spectrum, rebuilt = legendre_call(
            highest, start, band, wavenumbers, values, gathered, padded, spectrum
        )
        leaving = rebuilt.reshape(count, groups * bands, 2, LANES).transpose(1, 0, 2, 3)
        message = exchange(leaving)
        returned.append(message.reshape(groups, bands * count * 2, LANES))
    restored = inverse_call(length, fields, pair_ids, returned, table)
    return (
        spectrum.reshape(local_pairs, 2, fields // groups, degrees),
        restored.T.reshape(1, 1, fields, length),
    )


def solution(mesh):
    placed = (
        P("fld", "band", None, None),
        P("fld", "band"),
        P("fld", "band", None),
        P("fld", "band", None),
        P(),
        P("band", "fld", None),
        P(),
    )
    return jax.shard_map(
        on_device,
        mesh=mesh,
        in_specs=placed,
        out_specs=(P("band", None, "fld", None), P("fld", "band", None, None)),
        check_vma=False,
    )
```

```python
import functools

import jax
import jax.numpy as jnp
from jax import lax
from jax.experimental import pallas as pl
from jax.experimental.pallas import tpu as pltpu
from jax.sharding import PartitionSpec as P

PI = 3.141592653589793
LANES = 128
STEP = 512
INVERSE_BLOCK = 656
STRIP = 64
VMEM_BYTES = 40 * 1024 * 1024
LARGE_VMEM_BYTES = 50_000_000
WHOLE_VMEM_BYTES = 58_000_000
CHUNKS = ((0, 5),)


def unit_circle(waves, points, count):
    inverse = 1.0 / count
    product = waves * points
    residue = product - jnp.round(product * inverse) * count
    half = residue * (inverse * PI)
    square = half * half
    sine = 1.0 / 6227020800.0
    for term in (-1.0 / 39916800.0, 1.0 / 362880.0, -1.0 / 5040.0, 1.0 / 120.0, -1.0 / 6.0, 1.0):
        sine = sine * square + term
    sine = sine * half
    cosine = 1.0 / 479001600.0
    for term in (-1.0 / 3628800.0, 1.0 / 40320.0, -1.0 / 720.0, 1.0 / 24.0, -0.5, 1.0):
        cosine = cosine * square + term
    return cosine * cosine - sine * sine, -2.0 * sine * cosine


def turn(state, step):
    cosine, sine = state
    return cosine * step[0] - sine * step[1], sine * step[0] + cosine * step[1]


def cycle_facts(length, highest, pair_ids, trims):
    first = 20 + 4 * pair_ids[0, 0]
    counts = (first, length - first)
    limits = [
        jnp.maximum(jnp.minimum(highest, count // 2 - 1) - trims[0, 0, cycle], 0)
        for cycle, count in enumerate(counts)
    ]
    return first, [c.astype(jnp.float32) for c in counts], [l.astype(jnp.float32) for l in limits]


def fill_table(axis, chosen, step_waves, facts, blocks, write):
    first, counts, limits = facts
    shape = chosen.shape
    lane = lax.broadcasted_iota(jnp.int32, shape, axis)
    straddle = first // LANES

    def begin(cycle, offset):
        state = unit_circle(chosen, (lane + offset).astype(jnp.float32), counts[cycle])
        kept = chosen <= limits[cycle]
        return tuple(jnp.where(kept, part, 0.0) for part in state)

    steps = step_waves(counts)

    def advance(cycle):
        def body(block, state):
            write(block, state)
            return turn(state, steps[cycle])

        return body

    state = lax.fori_loop(0, straddle, advance(0), begin(0, 0))
    offset = straddle * LANES - first
    later = begin(1, offset)
    before = lane + offset < 0
    write(straddle, tuple(jnp.where(before, old, new) for old, new in zip(state, later)))
    lax.fori_loop(straddle + 1, blocks, advance(1), turn(later, steps[1]))


def ordered_columns(chunk, stride, wavenumbers, raw, columns):
    total = wavenumbers.shape[0]
    raw[...] = jnp.broadcast_to(wavenumbers[...].astype(jnp.float32)[None, :], (LANES, total)).T
    target = 0
    for column in range(2):
        for pair in range(*chunk):
            columns[target:target + STRIP, :] = raw[pl.ds(2 * pair + column, STRIP, stride=stride), :]
            target += STRIP


def forward_kernel(highest, chunk, stride, pair_ids, trims, weights, wavenumbers, grid, packed, table, totals, raw, columns, rows):
    length, fields = grid.shape
    width = columns.shape[0]
    quarter = width // 2
    facts = cycle_facts(length, highest, pair_ids, trims)
    first, counts, _ = facts
    blocks = -(-length // LANES)
    ordered_columns(chunk, stride, wavenumbers, raw, columns)

    for strip in range(width // STRIP):
        chosen = columns[strip * STRIP:(strip + 1) * STRIP, :]

        def step_waves(counts):
            cycle_lane = lax.broadcasted_iota(jnp.int32, chosen.shape, 1)
            count = jnp.where(cycle_lane == 0, counts[0], counts[1])
            cosine, sine = unit_circle(chosen, float(LANES), count)
            return [
                tuple(jnp.broadcast_to(part[:, c:c + 1], chosen.shape) for part in (cosine, sine))
                for c in range(2)
            ]

        def write(block, state):
            for part in range(2):
                table[
                    part * width + strip * STRIP:part * width + (strip + 1) * STRIP,
                    pl.ds(pl.multiple_of(block * LANES, LANES), LANES),
                ] = state[part].astype(jnp.bfloat16)

        fill_table(1, chosen, step_waves, facts, blocks, write)

    split = -(-(length // 2) // STEP) * STEP
    totals[0] = jnp.zeros(totals.shape[1:], jnp.float32)
    totals[1] = jnp.dot(table[:, split:length], grid[split:, :], preferred_element_type=jnp.float32)
    position = lax.broadcasted_iota(jnp.int32, (STEP, fields), 0)
    for start in range(0, split, STEP):
        block = slice(start, start + STEP)
        data = grid[block, :]
        nothing = jnp.zeros_like(data)

        def add(cycle, data):
            totals[cycle] += jnp.dot(table[:, block], data, preferred_element_type=jnp.float32)

        @pl.when(first >= start + STEP)
        def _():
            add(0, data)

        @pl.when(first <= start)
        def _():
            add(1, data)

        @pl.when((first > start) & (first < start + STEP))
        def _():
            before = position + start < first
            add(0, jnp.where(before, data, nothing))
            add(1, jnp.where(before, nothing, data))

    share = LANES // 4
    for group in range(fields // share):
        lanes = slice(group * share, (group + 1) * share)
        for cycle in range(2):
            scale = jnp.full((1, LANES), weights[0, 0, cycle]) / counts[cycle]
            joined = jnp.concatenate(
                [totals[cycle, part * quarter:(part + 1) * quarter, lanes] for part in (0, 2, 1, 3)], axis=1
            )
            joined = joined * scale
            for pair in range(quarter // STRIP):
                rows[pl.ds(2 * pair + cycle, STRIP, stride=2 * quarter // STRIP), :] = (
                    joined[pair * STRIP:(pair + 1) * STRIP]
                )
        packed[group] = rows[...].astype(jnp.bfloat16)


def table_kernel(length, highest, stride, pair_ids, trims, wavenumbers, table, raw, columns):
    facts = cycle_facts(length, highest, pair_ids, trims)
    blocks = -(-length // LANES)
    base = 0
    for chunk in CHUNKS:
        width = 2 * STRIP * (chunk[1] - chunk[0])
        ordered_columns(chunk, stride, wavenumbers, raw, columns)
        for tile in range(width // LANES):
            chosen = columns[tile * LANES:(tile + 1) * LANES, :].T

            def step_waves(counts):
                return [
                    tuple(part[:1] for part in unit_circle(chosen[:8], float(LANES), count)) for count in counts
                ]

            def write(block, state):
                for part in range(2):
                    left = base + part * width + tile * LANES
                    table[pl.ds(pl.multiple_of(block * LANES, LANES), LANES), left:left + LANES] = (
                        state[part].astype(jnp.bfloat16)
                    )

            fill_table(0, chosen, step_waves, facts, blocks, write)
        base += 2 * width


def legendre_kernel(start, highest, band, wavenumbers, values, legendre, damping, *refs):
    spectrum, rebuilt = refs[-2:]
    groups, _, degrees, each = legendre.shape
    matrix = jnp.concatenate([legendre[group, 0] for group in range(groups)], axis=1)
    sums = jnp.dot(matrix, values[0], preferred_element_type=jnp.float32).T
    fields = sums.shape[0] // 2
    pair = band[0] + start + pl.program_id(0)
    first_wave = wavenumbers[2 * pair]
    second_wave = wavenumbers[2 * pair + 1]
    width = damping.shape[1]
    degree = lax.broadcasted_iota(jnp.int32, (1, width), 1)
    kept = degree < highest + 1 - first_wave
    upper = pltpu.roll(damping[...], lax.rem(width - first_wave, width), 1)
    lower = pltpu.roll(damping[...], 1, 1)
    factor = jnp.where(kept, upper[:1], lower[:1])[:, :degrees]
    head = jnp.broadcast_to(kept[:, :degrees], (fields, degrees))
    filtered = (jnp.where(head, sums[:fields], sums[fields:]) * factor).astype(jnp.bfloat16)
    spectrum[0] = filtered
    nothing = jnp.zeros_like(filtered)
    parts = jnp.concatenate([jnp.where(head, filtered, nothing), jnp.where(head, nothing, filtered)], axis=0)
    products = jnp.dot(parts, matrix, preferred_element_type=jnp.float32)
    row = lax.broadcasted_iota(jnp.int32, products.shape, 0)
    wave = jnp.where(row < fields, first_wave, second_wave)
    doubled = products * jnp.where(wave == 0, 1.0, 2.0)
    rebuilt[0] = doubled.astype(jnp.bfloat16).T


def inverse_kernel(chunks, pair_ids, *refs):
    values = refs[:chunks]
    table, restored, rows, factors = refs[chunks:]
    block = pl.program_id(0)
    first = 20 + 4 * pair_ids[0, 0]
    share = LANES // 4

    @pl.when(block == 0)
    def _():
        base = 0
        for chunk in values:
            groups, height, _ = chunk.shape
            quarter = height // 2
            for side in range(groups // 4):
                for near in range(4):
                    rows[near, :height] = chunk[4 * side + near].astype(jnp.float32)
                for cycle in range(2):
                    turned = [
                        jnp.concatenate(
                            [
                                rows[near, pl.ds(2 * pair + cycle, STRIP, stride=2 * quarter // STRIP), :]
                                for pair in range(quarter // STRIP)
                            ],
                            axis=0,
                        ).astype(jnp.bfloat16)
                        for near in range(4)
                    ]
                    for part in range(4):
                        source = (0, 2, 1, 3)[part] * share
                        factors[
                            cycle,
                            base + part * quarter:base + (part + 1) * quarter,
                            side * LANES:(side + 1) * LANES,
                        ] = jnp.concatenate([one[:, source:source + share] for one in turned], axis=1)
            base += 4 * quarter

    def product(cycle):
        return jnp.dot(table[...], factors[cycle], preferred_element_type=jnp.float32)

    start = block * INVERSE_BLOCK
    end = start + INVERSE_BLOCK

    @pl.when(end <= first)
    def _():
        restored[...] = product(0).astype(jnp.bfloat16)

    @pl.when(start >= first)
    def _():
        restored[...] = product(1).astype(jnp.bfloat16)

    @pl.when((start < first) & (end > first))
    def _():
        position = start + lax.broadcasted_iota(jnp.int32, restored.shape, 0)
        restored[...] = jnp.where(position < first, product(0), product(1)).astype(jnp.bfloat16)


SMEM = pl.BlockSpec(memory_space=pltpu.SMEM)
VMEM = pl.BlockSpec(memory_space=pltpu.VMEM)


def parameters(*semantics, limit=VMEM_BYTES):
    return pltpu.CompilerParams(dimension_semantics=semantics or None, vmem_limit_bytes=limit)


def forward_call(highest, chunk, stride, pair_ids, trims, weights, wavenumbers, points):
    length, fields = points.shape
    width = 2 * STRIP * (chunk[1] - chunk[0])
    blocks = -(-length // LANES)
    return pl.pallas_call(
        functools.partial(forward_kernel, highest, chunk, stride),
        in_specs=[SMEM, SMEM, SMEM, VMEM, VMEM],
        out_specs=VMEM,
        out_shape=jax.ShapeDtypeStruct((4 * fields // LANES, width, LANES), jnp.bfloat16),
        scratch_shapes=[
            pltpu.VMEM((2 * width, blocks * LANES), jnp.bfloat16),
            pltpu.VMEM((2, 2 * width, fields), jnp.float32),
            pltpu.VMEM((wavenumbers.shape[0], LANES), jnp.float32),
            pltpu.VMEM((width, LANES), jnp.float32),
            pltpu.VMEM((width, LANES), jnp.float32),
        ],
        compiler_params=parameters(limit=WHOLE_VMEM_BYTES),
        cost_estimate=pl.CostEstimate(
            flops=2 * length * fields * 2 * width, bytes_accessed=length * fields * 2, transcendentals=0
        ),
        name="forward_dft",
    )(pair_ids, trims, weights, wavenumbers, points)


def table_call(highest, length, stride, pair_ids, trims, wavenumbers):
    blocks = -(-length // LANES)
    total = 2 * wavenumbers.shape[0]
    return pl.pallas_call(
        functools.partial(table_kernel, length, highest, stride),
        in_specs=[SMEM, SMEM, VMEM],
        out_specs=VMEM,
        out_shape=jax.ShapeDtypeStruct((blocks * LANES, total), jnp.bfloat16),
        scratch_shapes=[
            pltpu.VMEM((wavenumbers.shape[0], LANES), jnp.float32),
            pltpu.VMEM((wavenumbers.shape[0], LANES), jnp.float32),
        ],
        compiler_params=parameters(),
        cost_estimate=pl.CostEstimate(flops=8 * length * total, bytes_accessed=2 * length * total, transcendentals=0),
        name="inverse_table",
    )(pair_ids, trims, wavenumbers)


def legendre_call(highest, start, band, wavenumbers, values, gathered, damping, spectrum):
    groups, local_pairs, degrees, each = gathered.shape
    count, cycles, _ = values.shape
    fields = LANES // 2
    previous = [] if spectrum is None else [spectrum]
    return pl.pallas_call(
        functools.partial(legendre_kernel, start, highest),
        grid=(count,),
        in_specs=[
            SMEM,
            SMEM,
            pl.BlockSpec((1, cycles, LANES), lambda q: (q, 0, 0)),
            pl.BlockSpec((groups, 1, degrees, each), lambda q: (0, q + start, 0, 0)),
            pl.BlockSpec(damping.shape, lambda q: (0, 0)),
        ]
        + [pl.BlockSpec(memory_space=pl.ANY)] * len(previous),
        out_specs=[
            pl.BlockSpec((1, fields, degrees), lambda q: (q + start, 0, 0)),
            pl.BlockSpec((1, cycles, LANES), lambda q: (q, 0, 0)),
        ],
        out_shape=[
            jax.ShapeDtypeStruct((local_pairs, fields, degrees), jnp.bfloat16),
            jax.ShapeDtypeStruct((count, cycles, LANES), jnp.bfloat16),
        ],
        input_output_aliases={5: 0} if previous else {},
        compiler_params=parameters("arbitrary", limit=LARGE_VMEM_BYTES),
        cost_estimate=pl.CostEstimate(
            flops=4 * count * cycles * LANES * degrees,
            bytes_accessed=2 * count * cycles * degrees,
            transcendentals=0,
        ),
        name="legendre_both_ways",
    )(band, wavenumbers, values, gathered, damping, *previous)


def inverse_call(length, fields, pair_ids, values, table):
    blocks = -(-length // INVERSE_BLOCK)
    total = table.shape[1]
    return pl.pallas_call(
        functools.partial(inverse_kernel, len(values)),
        grid=(blocks,),
        in_specs=[SMEM]
        + [pl.BlockSpec(one.shape, lambda i: (0, 0, 0)) for one in values]
        + [pl.BlockSpec((INVERSE_BLOCK, total), lambda i: (i, 0))],
        out_specs=pl.BlockSpec((INVERSE_BLOCK, fields), lambda i: (i, 0)),
        out_shape=jax.ShapeDtypeStruct((length, fields), jnp.bfloat16),
        scratch_shapes=[
            pltpu.VMEM((4, max(one.shape[1] for one in values), LANES), jnp.float32),
            pltpu.VMEM((2, total, fields), jnp.bfloat16),
        ],
        compiler_params=parameters("arbitrary", limit=LARGE_VMEM_BYTES),
        cost_estimate=pl.CostEstimate(
            flops=2 * length * fields * total, bytes_accessed=2 * length * (fields + total), transcendentals=0
        ),
        name="inverse_dft",
    )(pair_ids, *values, table)


def exchange(message):
    return lax.all_to_all(message, ("fld", "band"), split_axis=0, concat_axis=0, tiled=True)


def on_device(grid, pair_ids, trims, weights, wavenumbers, legendre, damping):
    fields, length = grid.shape[2:]
    columns = wavenumbers.shape[0]
    highest = columns - 1
    local_pairs, local_cycles, degrees = legendre.shape
    groups = lax.axis_size("fld")
    bands = lax.axis_size("band")
    gathered = lax.all_gather(legendre.swapaxes(1, 2), "fld")
    points = grid[0, 0].T
    stride = 2 * local_pairs
    padding = -(-degrees // LANES) * LANES - columns
    padded = jnp.broadcast_to(jnp.pad(damping, (0, padding))[None, :], (8, columns + padding))
    band = (lax.axis_index("band") * local_pairs).astype(jnp.int32).reshape(1)

    arrived = []
    for chunk in CHUNKS:
        packed = forward_call(highest, chunk, stride, pair_ids, trims, weights, wavenumbers, points)
        arrived.append(exchange(packed.reshape(groups * bands, chunk[1] - chunk[0], 2, LANES)))
    table = table_call(highest, length, stride, pair_ids, trims, wavenumbers)
    spectrum = None
    returned = []
    for (start, end), message in zip(CHUNKS, arrived):
        count = end - start
        values = message.transpose(1, 0, 2, 3).reshape(count, groups * local_cycles, LANES)
        spectrum, rebuilt = legendre_call(
            highest, start, band, wavenumbers, values, gathered, padded, spectrum
        )
        leaving = rebuilt.reshape(count, groups * bands, 2, LANES).transpose(1, 0, 2, 3)
        message = exchange(leaving)
        returned.append(message.reshape(groups, bands * count * 2, LANES))
    restored = inverse_call(length, fields, pair_ids, returned, table)
    return (
        spectrum.reshape(local_pairs, 2, fields // groups, degrees),
        restored.T.reshape(1, 1, fields, length),
    )


def solution(mesh):
    placed = (
        P("fld", "band", None, None),
        P("fld", "band"),
        P("fld", "band", None),
        P("fld", "band", None),
        P(),
        P("band", "fld", None),
        P(),
    )
    return jax.shard_map(
        on_device,
        mesh=mesh,
        in_specs=placed,
        out_specs=(P("band", None, "fld", None), P("fld", "band", None, None)),
        check_vma=False,
    )
```

```python
import functools

import jax
import jax.numpy as jnp
from jax import lax
from jax.experimental import pallas as pl
from jax.experimental.pallas import tpu as pltpu
from jax.sharding import PartitionSpec as P

PI = 3.141592653589793
LANES = 128
STEP = 512
INVERSE_BLOCK = 656
STRIP = 64
VMEM_BYTES = 40 * 1024 * 1024
LARGE_VMEM_BYTES = 50_000_000
WHOLE_VMEM_BYTES = 58_000_000
CHUNKS = ((0, 5),)


def unit_circle(waves, points, count):
    inverse = 1.0 / count
    product = waves * points
    residue = product - jnp.round(product * inverse) * count
    half = residue * (inverse * PI)
    square = half * half
    sine = 1.0 / 6227020800.0
    for term in (-1.0 / 39916800.0, 1.0 / 362880.0, -1.0 / 5040.0, 1.0 / 120.0, -1.0 / 6.0, 1.0):
        sine = sine * square + term
    sine = sine * half
    cosine = 1.0 / 479001600.0
    for term in (-1.0 / 3628800.0, 1.0 / 40320.0, -1.0 / 720.0, 1.0 / 24.0, -0.5, 1.0):
        cosine = cosine * square + term
    return cosine * cosine - sine * sine, -2.0 * sine * cosine


def turn(state, step):
    cosine, sine = state
    return cosine * step[0] - sine * step[1], sine * step[0] + cosine * step[1]


def cycle_facts(length, highest, pair_ids, trims):
    first = 20 + 4 * pair_ids[0, 0]
    counts = (first, length - first)
    limits = [
        jnp.maximum(jnp.minimum(highest, count // 2 - 1) - trims[0, 0, cycle], 0)
        for cycle, count in enumerate(counts)
    ]
    return first, [c.astype(jnp.float32) for c in counts], [l.astype(jnp.float32) for l in limits]


def fill_table(axis, chosen, step_waves, facts, blocks, write):
    first, counts, limits = facts
    shape = chosen.shape
    lane = lax.broadcasted_iota(jnp.int32, shape, axis)
    straddle = first // LANES

    def begin(cycle, offset):
        state = unit_circle(chosen, (lane + offset).astype(jnp.float32), counts[cycle])
        kept = chosen <= limits[cycle]
        return tuple(jnp.where(kept, part, 0.0) for part in state)

    steps = step_waves(counts)

    def advance(cycle):
        def body(block, state):
            write(block, state)
            return turn(state, steps[cycle])

        return body

    state = lax.fori_loop(0, straddle, advance(0), begin(0, 0))
    offset = straddle * LANES - first
    later = begin(1, offset)
    before = lane + offset < 0
    write(straddle, tuple(jnp.where(before, old, new) for old, new in zip(state, later)))
    lax.fori_loop(straddle + 1, blocks, advance(1), turn(later, steps[1]))


def ordered_columns(chunk, stride, wavenumbers, raw, columns):
    total = wavenumbers.shape[0]
    raw[...] = jnp.broadcast_to(wavenumbers[...].astype(jnp.float32)[None, :], (LANES, total)).T
    target = 0
    for column in range(2):
        for pair in range(*chunk):
            columns[target:target + STRIP, :] = raw[pl.ds(2 * pair + column, STRIP, stride=stride), :]
            target += STRIP


def forward_kernel(highest, chunk, stride, pair_ids, trims, weights, wavenumbers, grid_hbm, packed_hbm,
                   grid, packed, table, totals, raw, columns, rows, sems):
    length, fields = grid.shape
    width = columns.shape[0]
    arriving = pltpu.make_async_copy(grid_hbm, grid, sems.at[packed.shape[0]])
    arriving.start()
    quarter = width // 2
    facts = cycle_facts(length, highest, pair_ids, trims)
    first, counts, _ = facts
    blocks = -(-length // LANES)
    ordered_columns(chunk, stride, wavenumbers, raw, columns)

    for strip in range(width // STRIP):
        chosen = columns[strip * STRIP:(strip + 1) * STRIP, :]

        def step_waves(counts):
            cycle_lane = lax.broadcasted_iota(jnp.int32, chosen.shape, 1)
            count = jnp.where(cycle_lane == 0, counts[0], counts[1])
            cosine, sine = unit_circle(chosen, float(LANES), count)
            return [
                tuple(jnp.broadcast_to(part[:, c:c + 1], chosen.shape) for part in (cosine, sine))
                for c in range(2)
            ]

        def write(block, state):
            for part in range(2):
                table[
                    part * width + strip * STRIP:part * width + (strip + 1) * STRIP,
                    pl.ds(pl.multiple_of(block * LANES, LANES), LANES),
                ] = state[part].astype(jnp.bfloat16)

        fill_table(1, chosen, step_waves, facts, blocks, write)

    arriving.wait()
    split = -(-(length // 2) // STEP) * STEP
    totals[0] = jnp.zeros(totals.shape[1:], jnp.float32)
    totals[1] = jnp.dot(table[:, split:length], grid[split:, :], preferred_element_type=jnp.float32)
    position = lax.broadcasted_iota(jnp.int32, (STEP, fields), 0)
    for start in range(0, split, STEP):
        block = slice(start, start + STEP)
        data = grid[block, :]
        nothing = jnp.zeros_like(data)

        def add(cycle, data):
            totals[cycle] += jnp.dot(table[:, block], data, preferred_element_type=jnp.float32)

        @pl.when(first >= start + STEP)
        def _():
            add(0, data)

        @pl.when(first <= start)
        def _():
            add(1, data)

        @pl.when((first > start) & (first < start + STEP))
        def _():
            before = position + start < first
            add(0, jnp.where(before, data, nothing))
            add(1, jnp.where(before, nothing, data))

    share = LANES // 4
    leaving = []
    for group in range(fields // share):
        lanes = slice(group * share, (group + 1) * share)
        for cycle in range(2):
            scale = jnp.full((1, LANES), weights[0, 0, cycle]) / counts[cycle]
            joined = jnp.concatenate(
                [totals[cycle, part * quarter:(part + 1) * quarter, lanes] for part in (0, 2, 1, 3)], axis=1
            )
            joined = joined * scale
            for pair in range(quarter // STRIP):
                rows[pl.ds(2 * pair + cycle, STRIP, stride=2 * quarter // STRIP), :] = (
                    joined[pair * STRIP:(pair + 1) * STRIP]
                )
        packed[group] = rows[...].astype(jnp.bfloat16)
        leaving.append(pltpu.make_async_copy(packed.at[group], packed_hbm.at[group], sems.at[group]))
        leaving[-1].start()
    for copy in leaving:
        copy.wait()


def table_kernel(length, highest, stride, pair_ids, trims, wavenumbers, table, raw, columns):
    facts = cycle_facts(length, highest, pair_ids, trims)
    blocks = -(-length // LANES)
    base = 0
    for chunk in CHUNKS:
        width = 2 * STRIP * (chunk[1] - chunk[0])
        ordered_columns(chunk, stride, wavenumbers, raw, columns)
        for tile in range(width // LANES):
            chosen = columns[tile * LANES:(tile + 1) * LANES, :].T

            def step_waves(counts):
                return [
                    tuple(part[:1] for part in unit_circle(chosen[:8], float(LANES), count)) for count in counts
                ]

            def write(block, state):
                for part in range(2):
                    left = base + part * width + tile * LANES
                    table[pl.ds(pl.multiple_of(block * LANES, LANES), LANES), left:left + LANES] = (
                        state[part].astype(jnp.bfloat16)
                    )

            fill_table(0, chosen, step_waves, facts, blocks, write)
        base += 2 * width


def legendre_kernel(start, highest, band, wavenumbers, values, legendre, damping, *refs):
    spectrum, rebuilt = refs[-2:]
    groups, _, degrees, each = legendre.shape
    matrix = jnp.concatenate([legendre[group, 0] for group in range(groups)], axis=1)
    rows = (groups * each, LANES)
    sums = jnp.dot(matrix, values.reshape(*rows)[...], preferred_element_type=jnp.float32).T
    fields = sums.shape[0] // 2
    pair = band[0] + start + pl.program_id(0)
    first_wave = wavenumbers[2 * pair]
    second_wave = wavenumbers[2 * pair + 1]
    width = damping.shape[1]
    degree = lax.broadcasted_iota(jnp.int32, (1, width), 1)
    kept = degree < highest + 1 - first_wave
    upper = pltpu.roll(damping[...], lax.rem(width - first_wave, width), 1)
    lower = pltpu.roll(damping[...], 1, 1)
    factor = jnp.where(kept, upper[:1], lower[:1])[:, :degrees]
    head = jnp.broadcast_to(kept[:, :degrees], (fields, degrees))
    filtered = (jnp.where(head, sums[:fields], sums[fields:]) * factor).astype(jnp.bfloat16)
    spectrum[0] = filtered
    nothing = jnp.zeros_like(filtered)
    parts = jnp.concatenate([jnp.where(head, filtered, nothing), jnp.where(head, nothing, filtered)], axis=0)
    products = jnp.dot(parts, matrix, preferred_element_type=jnp.float32)
    row = lax.broadcasted_iota(jnp.int32, products.shape, 0)
    wave = jnp.where(row < fields, first_wave, second_wave)
    doubled = products * jnp.where(wave == 0, 1.0, 2.0)
    rebuilt.reshape(*rows)[...] = doubled.astype(jnp.bfloat16).T


def inverse_kernel(chunks, pair_ids, *refs):
    values = refs[:chunks]
    table_hbm, restored, table, rows, factors, sems = refs[chunks:]
    block = pl.program_id(0)
    first = 20 + 4 * pair_ids[0, 0]
    share = LANES // 4

    def arriving(block):
        part = pl.ds(pl.multiple_of(block * INVERSE_BLOCK, 16), INVERSE_BLOCK)
        return pltpu.make_async_copy(table_hbm.at[part, :], table.at[part, :], sems.at[block])

    @pl.when(block == 0)
    def _():
        for one in range(sems.shape[0]):
            arriving(one).start()
        base = 0
        for chunk in values:
            groups, height, _ = chunk.shape
            quarter = height // 2
            for side in range(groups // 4):
                for near in range(4):
                    rows[near, :height] = chunk[4 * side + near].astype(jnp.float32)
                for cycle in range(2):
                    turned = [
                        jnp.concatenate(
                            [
                                rows[near, pl.ds(2 * pair + cycle, STRIP, stride=2 * quarter // STRIP), :]
                                for pair in range(quarter // STRIP)
                            ],
                            axis=0,
                        ).astype(jnp.bfloat16)
                        for near in range(4)
                    ]
                    for part in range(4):
                        source = (0, 2, 1, 3)[part] * share
                        factors[
                            cycle,
                            base + part * quarter:base + (part + 1) * quarter,
                            side * LANES:(side + 1) * LANES,
                        ] = jnp.concatenate([one[:, source:source + share] for one in turned], axis=1)
            base += 4 * quarter

    arriving(block).wait()
    start = pl.multiple_of(block * INVERSE_BLOCK, 16)

    def product(cycle):
        return jnp.dot(
            table[pl.ds(start, INVERSE_BLOCK), :], factors[cycle], preferred_element_type=jnp.float32
        )

    end = start + INVERSE_BLOCK

    @pl.when(end <= first)
    def _():
        restored[...] = product(0).astype(jnp.bfloat16)

    @pl.when(start >= first)
    def _():
        restored[...] = product(1).astype(jnp.bfloat16)

    @pl.when((start < first) & (end > first))
    def _():
        position = start + lax.broadcasted_iota(jnp.int32, restored.shape, 0)
        restored[...] = jnp.where(position < first, product(0), product(1)).astype(jnp.bfloat16)


SMEM = pl.BlockSpec(memory_space=pltpu.SMEM)
VMEM = pl.BlockSpec(memory_space=pltpu.VMEM)


def parameters(*semantics, limit=VMEM_BYTES):
    return pltpu.CompilerParams(dimension_semantics=semantics or None, vmem_limit_bytes=limit)


def forward_call(highest, chunk, stride, pair_ids, trims, weights, wavenumbers, points):
    length, fields = points.shape
    width = 2 * STRIP * (chunk[1] - chunk[0])
    blocks = -(-length // LANES)
    groups = 4 * fields // LANES
    return pl.pallas_call(
        functools.partial(forward_kernel, highest, chunk, stride),
        in_specs=[SMEM, SMEM, SMEM, VMEM, pl.BlockSpec(memory_space=pl.ANY)],
        out_specs=pl.BlockSpec(memory_space=pl.ANY),
        out_shape=jax.ShapeDtypeStruct((groups, width, LANES), jnp.bfloat16),
        scratch_shapes=[
            pltpu.VMEM((length, fields), jnp.bfloat16),
            pltpu.VMEM((groups, width, LANES), jnp.bfloat16),
            pltpu.VMEM((2 * width, blocks * LANES), jnp.bfloat16),
            pltpu.VMEM((2, 2 * width, fields), jnp.float32),
            pltpu.VMEM((wavenumbers.shape[0], LANES), jnp.float32),
            pltpu.VMEM((width, LANES), jnp.float32),
            pltpu.VMEM((width, LANES), jnp.float32),
            pltpu.SemaphoreType.DMA((groups + 1,)),
        ],
        compiler_params=parameters(limit=WHOLE_VMEM_BYTES),
        cost_estimate=pl.CostEstimate(
            flops=2 * length * fields * 2 * width, bytes_accessed=length * fields * 2, transcendentals=0
        ),
        name="forward_dft",
    )(pair_ids, trims, weights, wavenumbers, points)


def table_call(highest, length, stride, pair_ids, trims, wavenumbers):
    blocks = -(-length // LANES)
    total = 2 * wavenumbers.shape[0]
    return pl.pallas_call(
        functools.partial(table_kernel, length, highest, stride),
        in_specs=[SMEM, SMEM, VMEM],
        out_specs=VMEM,
        out_shape=jax.ShapeDtypeStruct((blocks * LANES, total), jnp.bfloat16),
        scratch_shapes=[
            pltpu.VMEM((wavenumbers.shape[0], LANES), jnp.float32),
            pltpu.VMEM((wavenumbers.shape[0], LANES), jnp.float32),
        ],
        compiler_params=parameters(),
        cost_estimate=pl.CostEstimate(flops=8 * length * total, bytes_accessed=2 * length * total, transcendentals=0),
        name="inverse_table",
    )(pair_ids, trims, wavenumbers)


def legendre_call(highest, start, band, wavenumbers, values, gathered, damping, spectrum):
    groups, local_pairs, degrees, each = gathered.shape
    cycles = groups * each
    count = values.shape[1]
    pair_block = pl.BlockSpec((cycles // 2, 1, 2, LANES), lambda q: (0, q, 0, 0))
    fields = LANES // 2
    previous = [] if spectrum is None else [spectrum]
    return pl.pallas_call(
        functools.partial(legendre_kernel, start, highest),
        grid=(count,),
        in_specs=[
            SMEM,
            SMEM,
            pair_block,
            pl.BlockSpec((groups, 1, degrees, each), lambda q: (0, q + start, 0, 0)),
            pl.BlockSpec(damping.shape, lambda q: (0, 0)),
        ]
        + [pl.BlockSpec(memory_space=pl.ANY)] * len(previous),
        out_specs=[
            pl.BlockSpec((1, fields, degrees), lambda q: (q + start, 0, 0)),
            pair_block,
        ],
        out_shape=[
            jax.ShapeDtypeStruct((local_pairs, fields, degrees), jnp.bfloat16),
            jax.ShapeDtypeStruct(values.shape, jnp.bfloat16),
        ],
        input_output_aliases={5: 0} if previous else {},
        compiler_params=parameters("arbitrary", limit=LARGE_VMEM_BYTES),
        cost_estimate=pl.CostEstimate(
            flops=4 * count * cycles * LANES * degrees,
            bytes_accessed=2 * count * cycles * degrees,
            transcendentals=0,
        ),
        name="legendre_both_ways",
    )(band, wavenumbers, values, gathered, damping, *previous)


def inverse_call(length, fields, pair_ids, values, table):
    blocks = -(-length // INVERSE_BLOCK)
    total = table.shape[1]
    return pl.pallas_call(
        functools.partial(inverse_kernel, len(values)),
        grid=(blocks,),
        in_specs=[SMEM]
        + [pl.BlockSpec(one.shape, lambda i: (0, 0, 0)) for one in values]
        + [pl.BlockSpec(memory_space=pl.ANY)],
        out_specs=pl.BlockSpec((INVERSE_BLOCK, fields), lambda i: (i, 0)),
        out_shape=jax.ShapeDtypeStruct((length, fields), jnp.bfloat16),
        scratch_shapes=[
            pltpu.VMEM((blocks * INVERSE_BLOCK, total), jnp.bfloat16),
            pltpu.VMEM((4, max(one.shape[1] for one in values), LANES), jnp.float32),
            pltpu.VMEM((2, total, fields), jnp.bfloat16),
            pltpu.SemaphoreType.DMA((blocks,)),
        ],
        compiler_params=parameters("arbitrary", limit=LARGE_VMEM_BYTES),
        cost_estimate=pl.CostEstimate(
            flops=2 * length * fields * total, bytes_accessed=2 * length * (fields + total), transcendentals=0
        ),
        name="inverse_dft",
    )(pair_ids, *values, table)


def exchange(message):
    return lax.all_to_all(message, ("fld", "band"), split_axis=0, concat_axis=0, tiled=True)


def on_device(grid, pair_ids, trims, weights, wavenumbers, legendre, damping):
    fields, length = grid.shape[2:]
    columns = wavenumbers.shape[0]
    highest = columns - 1
    local_pairs, local_cycles, degrees = legendre.shape
    groups = lax.axis_size("fld")
    bands = lax.axis_size("band")
    gathered = lax.all_gather(legendre.swapaxes(1, 2), "fld")
    points = grid[0, 0].T
    stride = 2 * local_pairs
    padding = -(-degrees // LANES) * LANES - columns
    padded = jnp.broadcast_to(jnp.pad(damping, (0, padding))[None, :], (8, columns + padding))
    band = (lax.axis_index("band") * local_pairs).astype(jnp.int32).reshape(1)

    arrived = []
    for chunk in CHUNKS:
        packed = forward_call(highest, chunk, stride, pair_ids, trims, weights, wavenumbers, points)
        packed, trims = lax.optimization_barrier((packed, trims))
        arrived.append(exchange(packed.reshape(groups * bands, chunk[1] - chunk[0], 2, LANES)))
    table = table_call(highest, length, stride, pair_ids, trims, wavenumbers)
    spectrum = None
    returned = []
    for (start, end), message in zip(CHUNKS, arrived):
        spectrum, rebuilt = legendre_call(
            highest, start, band, wavenumbers, message, gathered, padded, spectrum
        )
        message = exchange(rebuilt)
        returned.append(message.reshape(groups, bands * (end - start) * 2, LANES))
    restored = inverse_call(length, fields, pair_ids, returned, table)
    return (
        spectrum.reshape(local_pairs, 2, fields // groups, degrees),
        restored.T.reshape(1, 1, fields, length),
    )


def solution(mesh):
    placed = (
        P("fld", "band", None, None),
        P("fld", "band"),
        P("fld", "band", None),
        P("fld", "band", None),
        P(),
        P("band", "fld", None),
        P(),
    )
    return jax.shard_map(
        on_device,
        mesh=mesh,
        in_specs=placed,
        out_specs=(P("band", None, "fld", None), P("fld", "band", None, None)),
        check_vma=False,
    )
```

```python
import functools

import jax
import jax.numpy as jnp
from jax import lax
from jax.experimental import pallas as pl
from jax.experimental.pallas import tpu as pltpu
from jax.sharding import PartitionSpec as P

PI = 3.141592653589793
LANES = 128
STEP = 512
INVERSE_BLOCK = 656
STRIP = 64
VMEM_BYTES = 40 * 1024 * 1024
LARGE_VMEM_BYTES = 52_000_000
WHOLE_VMEM_BYTES = 58_000_000
CHUNKS = ((0, 5),)
GATHERS = ((0, 3), (3, 5))


def unit_circle(waves, points, count):
    inverse = 1.0 / count
    product = waves * points
    residue = product - jnp.round(product * inverse) * count
    half = residue * (inverse * PI)
    square = half * half
    sine = 1.0 / 6227020800.0
    for term in (-1.0 / 39916800.0, 1.0 / 362880.0, -1.0 / 5040.0, 1.0 / 120.0, -1.0 / 6.0, 1.0):
        sine = sine * square + term
    sine = sine * half
    cosine = 1.0 / 479001600.0
    for term in (-1.0 / 3628800.0, 1.0 / 40320.0, -1.0 / 720.0, 1.0 / 24.0, -0.5, 1.0):
        cosine = cosine * square + term
    return cosine * cosine - sine * sine, -2.0 * sine * cosine


def turn(state, step):
    cosine, sine = state
    return cosine * step[0] - sine * step[1], sine * step[0] + cosine * step[1]


def cycle_facts(length, highest, pair_ids, trims):
    first = 20 + 4 * pair_ids[0, 0]
    counts = (first, length - first)
    limits = [
        jnp.maximum(jnp.minimum(highest, count // 2 - 1) - trims[0, 0, cycle], 0)
        for cycle, count in enumerate(counts)
    ]
    return first, [c.astype(jnp.float32) for c in counts], [l.astype(jnp.float32) for l in limits]


def fill_table(axis, chosen, step_waves, facts, blocks, write):
    first, counts, limits = facts
    shape = chosen.shape
    lane = lax.broadcasted_iota(jnp.int32, shape, axis)
    straddle = first // LANES

    def begin(cycle, offset):
        state = unit_circle(chosen, (lane + offset).astype(jnp.float32), counts[cycle])
        kept = chosen <= limits[cycle]
        return tuple(jnp.where(kept, part, 0.0) for part in state)

    steps = step_waves(counts)

    def advance(cycle):
        def body(block, state):
            write(block, state)
            return turn(state, steps[cycle])

        return body

    state = lax.fori_loop(0, straddle, advance(0), begin(0, 0))
    offset = straddle * LANES - first
    later = begin(1, offset)
    before = lane + offset < 0
    write(straddle, tuple(jnp.where(before, old, new) for old, new in zip(state, later)))
    lax.fori_loop(straddle + 1, blocks, advance(1), turn(later, steps[1]))


def ordered_columns(chunk, stride, wavenumbers, raw, columns):
    total = wavenumbers.shape[0]
    raw[...] = jnp.broadcast_to(wavenumbers[...].astype(jnp.float32)[None, :], (LANES, total)).T
    target = 0
    for column in range(2):
        for pair in range(*chunk):
            columns[target:target + STRIP, :] = raw[pl.ds(2 * pair + column, STRIP, stride=stride), :]
            target += STRIP


def forward_kernel(highest, chunk, stride, pair_ids, trims, weights, wavenumbers, grid_hbm, packed_hbm,
                   grid, packed, table, totals, raw, columns, rows, sems):
    length, fields = grid.shape
    width = columns.shape[0]
    arriving = pltpu.make_async_copy(grid_hbm, grid, sems.at[packed.shape[0]])
    arriving.start()
    quarter = width // 2
    facts = cycle_facts(length, highest, pair_ids, trims)
    first, counts, _ = facts
    blocks = -(-length // LANES)
    ordered_columns(chunk, stride, wavenumbers, raw, columns)

    for strip in range(width // STRIP):
        chosen = columns[strip * STRIP:(strip + 1) * STRIP, :]

        def step_waves(counts):
            cycle_lane = lax.broadcasted_iota(jnp.int32, chosen.shape, 1)
            count = jnp.where(cycle_lane == 0, counts[0], counts[1])
            cosine, sine = unit_circle(chosen, float(LANES), count)
            return [
                tuple(jnp.broadcast_to(part[:, c:c + 1], chosen.shape) for part in (cosine, sine))
                for c in range(2)
            ]

        def write(block, state):
            for part in range(2):
                table[
                    part * width + strip * STRIP:part * width + (strip + 1) * STRIP,
                    pl.ds(pl.multiple_of(block * LANES, LANES), LANES),
                ] = state[part].astype(jnp.bfloat16)

        fill_table(1, chosen, step_waves, facts, blocks, write)

    arriving.wait()
    split = -(-(length // 2) // STEP) * STEP
    totals[0] = jnp.zeros(totals.shape[1:], jnp.float32)
    totals[1] = jnp.dot(table[:, split:length], grid[split:, :], preferred_element_type=jnp.float32)
    position = lax.broadcasted_iota(jnp.int32, (STEP, fields), 0)
    for start in range(0, split, STEP):
        block = slice(start, start + STEP)
        data = grid[block, :]
        nothing = jnp.zeros_like(data)

        def add(cycle, data):
            totals[cycle] += jnp.dot(table[:, block], data, preferred_element_type=jnp.float32)

        @pl.when(first >= start + STEP)
        def _():
            add(0, data)

        @pl.when(first <= start)
        def _():
            add(1, data)

        @pl.when((first > start) & (first < start + STEP))
        def _():
            before = position + start < first
            add(0, jnp.where(before, data, nothing))
            add(1, jnp.where(before, nothing, data))

    share = LANES // 4
    leaving = []
    for group in range(fields // share):
        lanes = slice(group * share, (group + 1) * share)
        for cycle in range(2):
            scale = jnp.full((1, LANES), weights[0, 0, cycle]) / counts[cycle]
            joined = jnp.concatenate(
                [totals[cycle, part * quarter:(part + 1) * quarter, lanes] for part in (0, 2, 1, 3)], axis=1
            )
            joined = joined * scale
            for pair in range(quarter // STRIP):
                rows[pl.ds(2 * pair + cycle, STRIP, stride=2 * quarter // STRIP), :] = (
                    joined[pair * STRIP:(pair + 1) * STRIP]
                )
        packed[group] = rows[...].astype(jnp.bfloat16)
        leaving.append(pltpu.make_async_copy(packed.at[group], packed_hbm.at[group], sems.at[group]))
        leaving[-1].start()
    for copy in leaving:
        copy.wait()


def table_kernel(length, highest, stride, pair_ids, trims, wavenumbers, table, raw, columns):
    facts = cycle_facts(length, highest, pair_ids, trims)
    blocks = -(-length // LANES)
    base = 0
    for chunk in CHUNKS:
        width = 2 * STRIP * (chunk[1] - chunk[0])
        ordered_columns(chunk, stride, wavenumbers, raw, columns)
        for tile in range(width // LANES):
            chosen = columns[tile * LANES:(tile + 1) * LANES, :].T

            def step_waves(counts):
                return [
                    tuple(part[:1] for part in unit_circle(chosen[:8], float(LANES), count)) for count in counts
                ]

            def write(block, state):
                for part in range(2):
                    left = base + part * width + tile * LANES
                    table[pl.ds(pl.multiple_of(block * LANES, LANES), LANES), left:left + LANES] = (
                        state[part].astype(jnp.bfloat16)
                    )

            fill_table(0, chosen, step_waves, facts, blocks, write)
        base += 2 * width


def legendre_kernel(start, highest, band, wavenumbers, values, legendre, damping, *refs):
    spectrum, rebuilt = refs[-2:]
    groups, _, degrees, each = legendre.shape
    matrix = jnp.concatenate([legendre[group, 0] for group in range(groups)], axis=1)
    rows = (groups * each, LANES)
    sums = jnp.dot(matrix, values.reshape(*rows)[...], preferred_element_type=jnp.float32).T
    fields = sums.shape[0] // 2
    pair = band[0] + start + pl.program_id(0)
    first_wave = wavenumbers[2 * pair]
    second_wave = wavenumbers[2 * pair + 1]
    width = damping.shape[1]
    degree = lax.broadcasted_iota(jnp.int32, (1, width), 1)
    kept = degree < highest + 1 - first_wave
    upper = pltpu.roll(damping[...], lax.rem(width - first_wave, width), 1)
    lower = pltpu.roll(damping[...], 1, 1)
    factor = jnp.where(kept, upper[:1], lower[:1])[:, :degrees]
    head = jnp.broadcast_to(kept[:, :degrees], (fields, degrees))
    filtered = (jnp.where(head, sums[:fields], sums[fields:]) * factor).astype(jnp.bfloat16)
    spectrum[0] = filtered
    nothing = jnp.zeros_like(filtered)
    parts = jnp.concatenate([jnp.where(head, filtered, nothing), jnp.where(head, nothing, filtered)], axis=0)
    products = jnp.dot(parts, matrix, preferred_element_type=jnp.float32)
    row = lax.broadcasted_iota(jnp.int32, products.shape, 0)
    wave = jnp.where(row < fields, first_wave, second_wave)
    doubled = products * jnp.where(wave == 0, 1.0, 2.0)
    rebuilt.reshape(*rows)[...] = doubled.astype(jnp.bfloat16).T


def inverse_kernel(chunks, pair_ids, *refs):
    values = refs[:chunks]
    table_hbm, restored, table, rows, factors, sems = refs[chunks:]
    block = pl.program_id(0)
    first = 20 + 4 * pair_ids[0, 0]
    share = LANES // 4

    def arriving(block):
        part = pl.ds(pl.multiple_of(block * INVERSE_BLOCK, 16), INVERSE_BLOCK)
        return pltpu.make_async_copy(table_hbm.at[part, :], table.at[part, :], sems.at[block])

    @pl.when(block == 0)
    def _():
        for one in range(sems.shape[0]):
            arriving(one).start()
        base = 0
        for chunk in values:
            groups, height, _ = chunk.shape
            quarter = height // 2
            for side in range(groups // 4):
                for near in range(4):
                    rows[near, :height] = chunk[4 * side + near].astype(jnp.float32)
                for cycle in range(2):
                    turned = [
                        jnp.concatenate(
                            [
                                rows[near, pl.ds(2 * pair + cycle, STRIP, stride=2 * quarter // STRIP), :]
                                for pair in range(quarter // STRIP)
                            ],
                            axis=0,
                        ).astype(jnp.bfloat16)
                        for near in range(4)
                    ]
                    for part in range(4):
                        source = (0, 2, 1, 3)[part] * share
                        factors[
                            cycle,
                            base + part * quarter:base + (part + 1) * quarter,
                            side * LANES:(side + 1) * LANES,
                        ] = jnp.concatenate([one[:, source:source + share] for one in turned], axis=1)
            base += 4 * quarter

    arriving(block).wait()
    start = pl.multiple_of(block * INVERSE_BLOCK, 16)

    def product(cycle):
        return jnp.dot(
            table[pl.ds(start, INVERSE_BLOCK), :], factors[cycle], preferred_element_type=jnp.float32
        )

    end = start + INVERSE_BLOCK

    @pl.when(end <= first)
    def _():
        restored[...] = product(0).astype(jnp.bfloat16)

    @pl.when(start >= first)
    def _():
        restored[...] = product(1).astype(jnp.bfloat16)

    @pl.when((start < first) & (end > first))
    def _():
        position = start + lax.broadcasted_iota(jnp.int32, restored.shape, 0)
        restored[...] = jnp.where(position < first, product(0), product(1)).astype(jnp.bfloat16)


SMEM = pl.BlockSpec(memory_space=pltpu.SMEM)
VMEM = pl.BlockSpec(memory_space=pltpu.VMEM)


def parameters(*semantics, limit=VMEM_BYTES):
    return pltpu.CompilerParams(dimension_semantics=semantics or None, vmem_limit_bytes=limit)


def forward_call(highest, chunk, stride, pair_ids, trims, weights, wavenumbers, points):
    length, fields = points.shape
    width = 2 * STRIP * (chunk[1] - chunk[0])
    blocks = -(-length // LANES)
    groups = 4 * fields // LANES
    return pl.pallas_call(
        functools.partial(forward_kernel, highest, chunk, stride),
        in_specs=[SMEM, SMEM, SMEM, VMEM, pl.BlockSpec(memory_space=pl.ANY)],
        out_specs=pl.BlockSpec(memory_space=pl.ANY),
        out_shape=jax.ShapeDtypeStruct((groups, width, LANES), jnp.bfloat16),
        scratch_shapes=[
            pltpu.VMEM((length, fields), jnp.bfloat16),
            pltpu.VMEM((groups, width, LANES), jnp.bfloat16),
            pltpu.VMEM((2 * width, blocks * LANES), jnp.bfloat16),
            pltpu.VMEM((2, 2 * width, fields), jnp.float32),
            pltpu.VMEM((wavenumbers.shape[0], LANES), jnp.float32),
            pltpu.VMEM((width, LANES), jnp.float32),
            pltpu.VMEM((width, LANES), jnp.float32),
            pltpu.SemaphoreType.DMA((groups + 1,)),
        ],
        compiler_params=parameters(limit=WHOLE_VMEM_BYTES),
        cost_estimate=pl.CostEstimate(
            flops=2 * length * fields * 2 * width, bytes_accessed=length * fields * 2, transcendentals=0
        ),
        name="forward_dft",
    )(pair_ids, trims, weights, wavenumbers, points)


def table_call(highest, length, stride, pair_ids, trims, wavenumbers):
    blocks = -(-length // LANES)
    total = 2 * wavenumbers.shape[0]
    return pl.pallas_call(
        functools.partial(table_kernel, length, highest, stride),
        in_specs=[SMEM, SMEM, VMEM],
        out_specs=VMEM,
        out_shape=jax.ShapeDtypeStruct((blocks * LANES, total), jnp.bfloat16),
        scratch_shapes=[
            pltpu.VMEM((wavenumbers.shape[0], LANES), jnp.float32),
            pltpu.VMEM((wavenumbers.shape[0], LANES), jnp.float32),
        ],
        compiler_params=parameters(),
        cost_estimate=pl.CostEstimate(flops=8 * length * total, bytes_accessed=2 * length * total, transcendentals=0),
        name="inverse_table",
    )(pair_ids, trims, wavenumbers)


def legendre_call(highest, start, band, wavenumbers, values, gathered, damping, previous):
    groups, count, degrees, each = gathered.shape
    cycles = groups * each
    local_pairs = values.shape[1]
    fields = LANES // 2
    pair_block = pl.BlockSpec((cycles // 2, 1, 2, LANES), lambda q: (0, q + start, 0, 0))
    return pl.pallas_call(
        functools.partial(legendre_kernel, start, highest),
        grid=(count,),
        in_specs=[
            SMEM,
            SMEM,
            pair_block,
            pl.BlockSpec((groups, 1, degrees, each), lambda q: (0, q, 0, 0)),
            pl.BlockSpec(damping.shape, lambda q: (0, 0)),
        ]
        + [pl.BlockSpec(memory_space=pl.ANY)] * len(previous),
        out_specs=[
            pl.BlockSpec((1, fields, degrees), lambda q: (q + start, 0, 0)),
            pair_block,
        ],
        out_shape=[
            jax.ShapeDtypeStruct((local_pairs, fields, degrees), jnp.bfloat16),
            jax.ShapeDtypeStruct(values.shape, jnp.bfloat16),
        ],
        input_output_aliases={5 + one: one for one in range(len(previous))},
        compiler_params=parameters("arbitrary", limit=LARGE_VMEM_BYTES),
        cost_estimate=pl.CostEstimate(
            flops=4 * count * cycles * LANES * degrees,
            bytes_accessed=2 * count * cycles * degrees,
            transcendentals=0,
        ),
        name="legendre_both_ways",
    )(band, wavenumbers, values, gathered, damping, *previous)


def inverse_call(length, fields, pair_ids, values, table):
    blocks = -(-length // INVERSE_BLOCK)
    total = table.shape[1]
    return pl.pallas_call(
        functools.partial(inverse_kernel, len(values)),
        grid=(blocks,),
        in_specs=[SMEM]
        + [pl.BlockSpec(one.shape, lambda i: (0, 0, 0)) for one in values]
        + [pl.BlockSpec(memory_space=pl.ANY)],
        out_specs=pl.BlockSpec((INVERSE_BLOCK, fields), lambda i: (i, 0)),
        out_shape=jax.ShapeDtypeStruct((length, fields), jnp.bfloat16),
        scratch_shapes=[
            pltpu.VMEM((blocks * INVERSE_BLOCK, total), jnp.bfloat16),
            pltpu.VMEM((4, max(one.shape[1] for one in values), LANES), jnp.float32),
            pltpu.VMEM((2, total, fields), jnp.bfloat16),
            pltpu.SemaphoreType.DMA((blocks,)),
        ],
        compiler_params=parameters("arbitrary", limit=LARGE_VMEM_BYTES),
        cost_estimate=pl.CostEstimate(
            flops=2 * length * fields * total, bytes_accessed=2 * length * (fields + total), transcendentals=0
        ),
        name="inverse_dft",
    )(pair_ids, *values, table)


def exchange(message):
    return lax.all_to_all(message, ("fld", "band"), split_axis=0, concat_axis=0, tiled=True)


def on_device(grid, pair_ids, trims, weights, wavenumbers, legendre, damping):
    fields, length = grid.shape[2:]
    columns = wavenumbers.shape[0]
    highest = columns - 1
    local_pairs, local_cycles, degrees = legendre.shape
    groups = lax.axis_size("fld")
    bands = lax.axis_size("band")
    gathered = [
        lax.all_gather(legendre[start:end].swapaxes(1, 2), "fld") for start, end in GATHERS
    ]
    points = grid[0, 0].T
    stride = 2 * local_pairs
    padding = -(-degrees // LANES) * LANES - columns
    padded = jnp.broadcast_to(jnp.pad(damping, (0, padding))[None, :], (8, columns + padding))
    band = (lax.axis_index("band") * local_pairs).astype(jnp.int32).reshape(1)

    arrived = []
    for chunk in CHUNKS:
        packed = forward_call(highest, chunk, stride, pair_ids, trims, weights, wavenumbers, points)
        packed, trims = lax.optimization_barrier((packed, trims))
        arrived.append(exchange(packed.reshape(groups * bands, chunk[1] - chunk[0], 2, LANES)))
    table = table_call(highest, length, stride, pair_ids, trims, wavenumbers)
    message = arrived[0]
    previous = []
    for (start, _), part in zip(GATHERS, gathered):
        previous = legendre_call(highest, start, band, wavenumbers, message, part, padded, previous)
    spectrum, rebuilt = previous
    returned = [exchange(rebuilt).reshape(groups, bands * local_pairs * 2, LANES)]
    restored = inverse_call(length, fields, pair_ids, returned, table)
    return (
        spectrum.reshape(local_pairs, 2, fields // groups, degrees),
        restored.T.reshape(1, 1, fields, length),
    )


def solution(mesh):
    placed = (
        P("fld", "band", None, None),
        P("fld", "band"),
        P("fld", "band", None),
        P("fld", "band", None),
        P(),
        P("band", "fld", None),
        P(),
    )
    return jax.shard_map(
        on_device,
        mesh=mesh,
        in_specs=placed,
        out_specs=(P("band", None, "fld", None), P("fld", "band", None, None)),
        check_vma=False,
    )
```

```python
import functools

import jax
import jax.numpy as jnp
from jax import lax
from jax.experimental import pallas as pl
from jax.experimental.pallas import tpu as pltpu
from jax.sharding import PartitionSpec as P

PI = 3.141592653589793
LANES = 128
STEP = 512
INVERSE_BLOCK = 672
STRIP = 64
VMEM_BYTES = 40 * 1024 * 1024
LARGE_VMEM_BYTES = 50_000_000
WHOLE_VMEM_BYTES = 58_000_000
CHUNKS = ((0, 5),)


def unit_circle(waves, points, count):
    inverse = 1.0 / count
    product = waves * points
    residue = product - jnp.round(product * inverse) * count
    half = residue * (inverse * PI)
    square = half * half
    sine = 1.0 / 6227020800.0
    for term in (-1.0 / 39916800.0, 1.0 / 362880.0, -1.0 / 5040.0, 1.0 / 120.0, -1.0 / 6.0, 1.0):
        sine = sine * square + term
    sine = sine * half
    cosine = 1.0 / 479001600.0
    for term in (-1.0 / 3628800.0, 1.0 / 40320.0, -1.0 / 720.0, 1.0 / 24.0, -0.5, 1.0):
        cosine = cosine * square + term
    return cosine * cosine - sine * sine, -2.0 * sine * cosine


def turn(state, step):
    cosine, sine = state
    return cosine * step[0] - sine * step[1], sine * step[0] + cosine * step[1]


def cycle_facts(length, highest, pair_ids, trims):
    first = 20 + 4 * pair_ids[0, 0]
    counts = (first, length - first)
    limits = [
        jnp.maximum(jnp.minimum(highest, count // 2 - 1) - trims[0, 0, cycle], 0)
        for cycle, count in enumerate(counts)
    ]
    return first, [c.astype(jnp.float32) for c in counts], [l.astype(jnp.float32) for l in limits]


def fill_table(axis, chosen, step_waves, facts, blocks, write):
    first, counts, limits = facts
    shape = chosen.shape
    lane = lax.broadcasted_iota(jnp.int32, shape, axis)
    straddle = first // LANES

    def begin(cycle, offset):
        state = unit_circle(chosen, (lane + offset).astype(jnp.float32), counts[cycle])
        kept = chosen <= limits[cycle]
        return tuple(jnp.where(kept, part, 0.0) for part in state)

    steps = step_waves(counts)

    def advance(cycle):
        def body(block, state):
            write(block, state)
            return turn(state, steps[cycle])

        return body

    state = lax.fori_loop(0, straddle, advance(0), begin(0, 0))
    offset = straddle * LANES - first
    later = begin(1, offset)
    before = lane + offset < 0
    write(straddle, tuple(jnp.where(before, old, new) for old, new in zip(state, later)))
    lax.fori_loop(straddle + 1, blocks, advance(1), turn(later, steps[1]))


def ordered_columns(chunk, stride, wavenumbers, raw, columns):
    total = wavenumbers.shape[0]
    raw[...] = jnp.broadcast_to(wavenumbers[...].astype(jnp.float32)[None, :], (LANES, total)).T
    target = 0
    for column in range(2):
        for pair in range(*chunk):
            columns[target:target + STRIP, :] = raw[pl.ds(2 * pair + column, STRIP, stride=stride), :]
            target += STRIP


def forward_kernel(highest, chunk, stride, pair_ids, trims, weights, wavenumbers, grid_hbm, packed_hbm,
                   grid, packed, table, totals, raw, columns, rows, sems):
    length, fields = grid.shape
    width = columns.shape[0]
    arriving = pltpu.make_async_copy(grid_hbm, grid, sems.at[packed.shape[0]])
    arriving.start()
    quarter = width // 2
    facts = cycle_facts(length, highest, pair_ids, trims)
    first, counts, _ = facts
    blocks = -(-length // LANES)
    ordered_columns(chunk, stride, wavenumbers, raw, columns)

    for strip in range(width // STRIP):
        chosen = columns[strip * STRIP:(strip + 1) * STRIP, :]

        def step_waves(counts):
            cycle_lane = lax.broadcasted_iota(jnp.int32, chosen.shape, 1)
            count = jnp.where(cycle_lane == 0, counts[0], counts[1])
            cosine, sine = unit_circle(chosen, float(LANES), count)
            return [
                tuple(jnp.broadcast_to(part[:, c:c + 1], chosen.shape) for part in (cosine, sine))
                for c in range(2)
            ]

        def write(block, state):
            for part in range(2):
                table[
                    part * width + strip * STRIP:part * width + (strip + 1) * STRIP,
                    pl.ds(pl.multiple_of(block * LANES, LANES), LANES),
                ] = state[part].astype(jnp.bfloat16)

        fill_table(1, chosen, step_waves, facts, blocks, write)

    arriving.wait()
    split = -(-(length // 2) // STEP) * STEP
    totals[0] = jnp.zeros(totals.shape[1:], jnp.float32)
    totals[1] = jnp.dot(table[:, split:length], grid[split:, :], preferred_element_type=jnp.float32)
    position = lax.broadcasted_iota(jnp.int32, (STEP, fields), 0)
    for start in range(0, split, STEP):
        block = slice(start, start + STEP)
        data = grid[block, :]
        nothing = jnp.zeros_like(data)

        def add(cycle, data):
            totals[cycle] += jnp.dot(table[:, block], data, preferred_element_type=jnp.float32)

        @pl.when(first >= start + STEP)
        def _():
            add(0, data)

        @pl.when(first <= start)
        def _():
            add(1, data)

        @pl.when((first > start) & (first < start + STEP))
        def _():
            before = position + start < first
            add(0, jnp.where(before, data, nothing))
            add(1, jnp.where(before, nothing, data))

    share = LANES // 4
    leaving = []
    for group in range(fields // share):
        lanes = slice(group * share, (group + 1) * share)
        for cycle in range(2):
            scale = jnp.full((1, LANES), weights[0, 0, cycle]) / counts[cycle]
            joined = jnp.concatenate(
                [totals[cycle, part * quarter:(part + 1) * quarter, lanes] for part in (0, 2, 1, 3)], axis=1
            )
            joined = joined * scale
            for pair in range(quarter // STRIP):
                rows[pl.ds(2 * pair + cycle, STRIP, stride=2 * quarter // STRIP), :] = (
                    joined[pair * STRIP:(pair + 1) * STRIP]
                )
        packed[group] = rows[...].astype(jnp.bfloat16)
        leaving.append(pltpu.make_async_copy(packed.at[group], packed_hbm.at[group], sems.at[group]))
        leaving[-1].start()
    for copy in leaving:
        copy.wait()


def table_kernel(length, highest, stride, pair_ids, trims, wavenumbers, table, raw, columns):
    facts = cycle_facts(length, highest, pair_ids, trims)
    blocks = -(-length // LANES)
    base = 0
    for chunk in CHUNKS:
        width = 2 * STRIP * (chunk[1] - chunk[0])
        ordered_columns(chunk, stride, wavenumbers, raw, columns)
        for tile in range(width // LANES):
            chosen = columns[tile * LANES:(tile + 1) * LANES, :].T

            def step_waves(counts):
                return [
                    tuple(part[:1] for part in unit_circle(chosen[:8], float(LANES), count)) for count in counts
                ]

            def write(block, state):
                for part in range(2):
                    left = base + part * width + tile * LANES
                    table[pl.ds(pl.multiple_of(block * LANES, LANES), LANES), left:left + LANES] = (
                        state[part].astype(jnp.bfloat16)
                    )

            fill_table(0, chosen, step_waves, facts, blocks, write)
        base += 2 * width


def legendre_kernel(start, highest, band, wavenumbers, values, legendre, damping, *refs):
    spectrum, rebuilt = refs[-2:]
    groups, _, degrees, each = legendre.shape

    def matrix(start, count):
        return jnp.concatenate([legendre[group, 0] for group in range(start, start + count)], axis=1)

    rows = (groups * each, LANES)
    sums = jnp.dot(matrix(0, groups), values.reshape(*rows)[...], preferred_element_type=jnp.float32).T
    fields = sums.shape[0] // 2
    pair = band[0] + start + pl.program_id(0)
    first_wave = wavenumbers[2 * pair]
    second_wave = wavenumbers[2 * pair + 1]
    width = damping.shape[1]
    degree = lax.broadcasted_iota(jnp.int32, (1, width), 1)
    kept = degree < highest + 1 - first_wave
    upper = pltpu.roll(damping[...], lax.rem(width - first_wave, width), 1)
    lower = pltpu.roll(damping[...], 1, 1)
    factor = jnp.where(kept, upper[:1], lower[:1])[:, :degrees]
    head = jnp.broadcast_to(kept[:, :degrees], (fields, degrees))
    filtered = (jnp.where(head, sums[:fields], sums[fields:]) * factor).astype(jnp.bfloat16)
    spectrum[0] = filtered
    nothing = jnp.zeros_like(filtered)
    doubled = [
        filtered * jnp.where(wave == 0, 1.0, 2.0).astype(jnp.bfloat16) for wave in (first_wave, second_wave)
    ]
    parts = jnp.concatenate([jnp.where(head, doubled[0], nothing), jnp.where(head, nothing, doubled[1])], axis=0)
    leaving = rebuilt.reshape(*rows)
    for start in range(0, groups, 2):
        products = jnp.dot(parts, matrix(start, 2), preferred_element_type=jnp.float32)
        leaving[start * each:(start + 2) * each, :] = products.astype(jnp.bfloat16).T


def inverse_kernel(chunks, pair_ids, *refs):
    values = refs[:chunks]
    table_hbm, restored, table, rows, factors, sems = refs[chunks:]
    block = pl.program_id(0)
    first = 20 + 4 * pair_ids[0, 0]
    share = LANES // 4

    def arriving(block):
        part = pl.ds(pl.multiple_of(block * INVERSE_BLOCK, 16), INVERSE_BLOCK)
        return pltpu.make_async_copy(table_hbm.at[part, :], table.at[part, :], sems.at[block])

    @pl.when(block == 0)
    def _():
        for one in range(sems.shape[0]):
            arriving(one).start()
        base = 0
        for chunk in values:
            groups, height, _ = chunk.shape
            quarter = height // 2
            for side in range(groups // 4):
                for near in range(4):
                    rows[near, :height] = chunk[4 * side + near].astype(jnp.float32)
                for cycle in range(2):
                    turned = [
                        jnp.concatenate(
                            [
                                rows[near, pl.ds(2 * pair + cycle, STRIP, stride=2 * quarter // STRIP), :]
                                for pair in range(quarter // STRIP)
                            ],
                            axis=0,
                        ).astype(jnp.bfloat16)
                        for near in range(4)
                    ]
                    for part in range(4):
                        source = (0, 2, 1, 3)[part] * share
                        factors[
                            cycle,
                            base + part * quarter:base + (part + 1) * quarter,
                            side * LANES:(side + 1) * LANES,
                        ] = jnp.concatenate([one[:, source:source + share] for one in turned], axis=1)
            base += 4 * quarter

    arriving(block).wait()
    half = INVERSE_BLOCK // 2
    for side in range(2):
        start = pl.multiple_of(block * INVERSE_BLOCK + side * half, 16)
        end = start + half
        target = slice(side * half, (side + 1) * half)

        def product(cycle):
            return jnp.dot(table[pl.ds(start, half), :], factors[cycle], preferred_element_type=jnp.float32)

        @pl.when(end <= first)
        def _():
            restored[target, :] = product(0).astype(jnp.bfloat16)

        @pl.when(start >= first)
        def _():
            restored[target, :] = product(1).astype(jnp.bfloat16)

        @pl.when((start < first) & (end > first))
        def _():
            position = start + lax.broadcasted_iota(jnp.int32, (half, restored.shape[1]), 0)
            restored[target, :] = jnp.where(position < first, product(0), product(1)).astype(jnp.bfloat16)


SMEM = pl.BlockSpec(memory_space=pltpu.SMEM)
VMEM = pl.BlockSpec(memory_space=pltpu.VMEM)


def parameters(*semantics, limit=VMEM_BYTES):
    return pltpu.CompilerParams(dimension_semantics=semantics or None, vmem_limit_bytes=limit)


def forward_call(highest, chunk, stride, pair_ids, trims, weights, wavenumbers, points):
    length, fields = points.shape
    width = 2 * STRIP * (chunk[1] - chunk[0])
    blocks = -(-length // LANES)
    groups = 4 * fields // LANES
    return pl.pallas_call(
        functools.partial(forward_kernel, highest, chunk, stride),
        in_specs=[SMEM, SMEM, SMEM, VMEM, pl.BlockSpec(memory_space=pl.ANY)],
        out_specs=pl.BlockSpec(memory_space=pl.ANY),
        out_shape=jax.ShapeDtypeStruct((groups, width, LANES), jnp.bfloat16),
        scratch_shapes=[
            pltpu.VMEM((length, fields), jnp.bfloat16),
            pltpu.VMEM((groups, width, LANES), jnp.bfloat16),
            pltpu.VMEM((2 * width, blocks * LANES), jnp.bfloat16),
            pltpu.VMEM((2, 2 * width, fields), jnp.float32),
            pltpu.VMEM((wavenumbers.shape[0], LANES), jnp.float32),
            pltpu.VMEM((width, LANES), jnp.float32),
            pltpu.VMEM((width, LANES), jnp.float32),
            pltpu.SemaphoreType.DMA((groups + 1,)),
        ],
        compiler_params=parameters(limit=WHOLE_VMEM_BYTES),
        cost_estimate=pl.CostEstimate(
            flops=2 * length * fields * 2 * width, bytes_accessed=length * fields * 2, transcendentals=0
        ),
        name="forward_dft",
    )(pair_ids, trims, weights, wavenumbers, points)


def table_call(highest, length, stride, pair_ids, trims, wavenumbers):
    blocks = -(-length // LANES)
    total = 2 * wavenumbers.shape[0]
    return pl.pallas_call(
        functools.partial(table_kernel, length, highest, stride),
        in_specs=[SMEM, SMEM, VMEM],
        out_specs=VMEM,
        out_shape=jax.ShapeDtypeStruct((blocks * LANES, total), jnp.bfloat16),
        scratch_shapes=[
            pltpu.VMEM((wavenumbers.shape[0], LANES), jnp.float32),
            pltpu.VMEM((wavenumbers.shape[0], LANES), jnp.float32),
        ],
        compiler_params=parameters(),
        cost_estimate=pl.CostEstimate(flops=8 * length * total, bytes_accessed=2 * length * total, transcendentals=0),
        name="inverse_table",
    )(pair_ids, trims, wavenumbers)


def legendre_call(highest, start, band, wavenumbers, values, gathered, damping, spectrum):
    groups, local_pairs, degrees, each = gathered.shape
    cycles = groups * each
    count = values.shape[1]
    pair_block = pl.BlockSpec((cycles // 2, 1, 2, LANES), lambda q: (0, q, 0, 0))
    fields = LANES // 2
    previous = [] if spectrum is None else [spectrum]
    return pl.pallas_call(
        functools.partial(legendre_kernel, start, highest),
        grid=(count,),
        in_specs=[
            SMEM,
            SMEM,
            pair_block,
            pl.BlockSpec((groups, 1, degrees, each), lambda q: (0, q + start, 0, 0)),
            pl.BlockSpec(damping.shape, lambda q: (0, 0)),
        ]
        + [pl.BlockSpec(memory_space=pl.ANY)] * len(previous),
        out_specs=[
            pl.BlockSpec((1, fields, degrees), lambda q: (q + start, 0, 0)),
            pair_block,
        ],
        out_shape=[
            jax.ShapeDtypeStruct((local_pairs, fields, degrees), jnp.bfloat16),
            jax.ShapeDtypeStruct(values.shape, jnp.bfloat16),
        ],
        input_output_aliases={5: 0} if previous else {},
        compiler_params=parameters("arbitrary", limit=LARGE_VMEM_BYTES),
        cost_estimate=pl.CostEstimate(
            flops=4 * count * cycles * LANES * degrees,
            bytes_accessed=2 * count * cycles * degrees,
            transcendentals=0,
        ),
        name="legendre_both_ways",
    )(band, wavenumbers, values, gathered, damping, *previous)


def inverse_call(length, fields, pair_ids, values, table):
    blocks = -(-length // INVERSE_BLOCK)
    total = table.shape[1]
    return pl.pallas_call(
        functools.partial(inverse_kernel, len(values)),
        grid=(blocks,),
        in_specs=[SMEM]
        + [pl.BlockSpec(one.shape, lambda i: (0, 0, 0)) for one in values]
        + [pl.BlockSpec(memory_space=pl.ANY)],
        out_specs=pl.BlockSpec((INVERSE_BLOCK, fields), lambda i: (i, 0)),
        out_shape=jax.ShapeDtypeStruct((length, fields), jnp.bfloat16),
        scratch_shapes=[
            pltpu.VMEM((blocks * INVERSE_BLOCK, total), jnp.bfloat16),
            pltpu.VMEM((4, max(one.shape[1] for one in values), LANES), jnp.float32),
            pltpu.VMEM((2, total, fields), jnp.bfloat16),
            pltpu.SemaphoreType.DMA((blocks,)),
        ],
        compiler_params=parameters("arbitrary", limit=LARGE_VMEM_BYTES),
        cost_estimate=pl.CostEstimate(
            flops=2 * length * fields * total, bytes_accessed=2 * length * (fields + total), transcendentals=0
        ),
        name="inverse_dft",
    )(pair_ids, *values, table)


def exchange(message):
    return lax.all_to_all(message, ("fld", "band"), split_axis=0, concat_axis=0, tiled=True)


def on_device(grid, pair_ids, trims, weights, wavenumbers, legendre, damping):
    fields, length = grid.shape[2:]
    columns = wavenumbers.shape[0]
    highest = columns - 1
    local_pairs, local_cycles, degrees = legendre.shape
    groups = lax.axis_size("fld")
    bands = lax.axis_size("band")
    gathered = lax.all_gather(legendre.swapaxes(1, 2), "fld")
    points = grid[0, 0].T
    stride = 2 * local_pairs
    padding = -(-degrees // LANES) * LANES - columns
    padded = jnp.broadcast_to(jnp.pad(damping, (0, padding))[None, :], (8, columns + padding))
    band = (lax.axis_index("band") * local_pairs).astype(jnp.int32).reshape(1)

    arrived = []
    for chunk in CHUNKS:
        packed = forward_call(highest, chunk, stride, pair_ids, trims, weights, wavenumbers, points)
        packed, trims = lax.optimization_barrier((packed, trims))
        arrived.append(exchange(packed.reshape(groups * bands, chunk[1] - chunk[0], 2, LANES)))
    table = table_call(highest, length, stride, pair_ids, trims, wavenumbers)
    spectrum = None
    returned = []
    for (start, end), message in zip(CHUNKS, arrived):
        spectrum, rebuilt = legendre_call(
            highest, start, band, wavenumbers, message, gathered, padded, spectrum
        )
        message = exchange(rebuilt)
        returned.append(message.reshape(groups, bands * (end - start) * 2, LANES))
    restored = inverse_call(length, fields, pair_ids, returned, table)
    return (
        spectrum.reshape(local_pairs, 2, fields // groups, degrees),
        restored.T.reshape(1, 1, fields, length),
    )


def solution(mesh):
    placed = (
        P("fld", "band", None, None),
        P("fld", "band"),
        P("fld", "band", None),
        P("fld", "band", None),
        P(),
        P("band", "fld", None),
        P(),
    )
    return jax.shard_map(
        on_device,
        mesh=mesh,
        in_specs=placed,
        out_specs=(P("band", None, "fld", None), P("fld", "band", None, None)),
        check_vma=False,
    )
```

```python
import functools

import jax
import jax.numpy as jnp
from jax import lax
from jax.experimental import pallas as pl
from jax.experimental.pallas import tpu as pltpu
from jax.sharding import PartitionSpec as P

PI = 3.141592653589793
LANES = 128
STEP = 512
INVERSE_BLOCK = 656
STRIP = 64
VMEM_BYTES = 40 * 1024 * 1024
LARGE_VMEM_BYTES = 50_000_000
WHOLE_VMEM_BYTES = 58_000_000
CHUNKS = ((0, 5),)


def unit_circle(waves, points, count):
    inverse = 1.0 / count
    product = waves * points
    residue = product - jnp.round(product * inverse) * count
    half = residue * (inverse * PI)
    square = half * half
    sine = 1.0 / 6227020800.0
    for term in (-1.0 / 39916800.0, 1.0 / 362880.0, -1.0 / 5040.0, 1.0 / 120.0, -1.0 / 6.0, 1.0):
        sine = sine * square + term
    sine = sine * half
    cosine = 1.0 / 479001600.0
    for term in (-1.0 / 3628800.0, 1.0 / 40320.0, -1.0 / 720.0, 1.0 / 24.0, -0.5, 1.0):
        cosine = cosine * square + term
    return cosine * cosine - sine * sine, -2.0 * sine * cosine


def turn(state, step):
    cosine, sine = state
    return cosine * step[0] - sine * step[1], sine * step[0] + cosine * step[1]


def cycle_facts(length, highest, pair_ids, trims):
    first = 20 + 4 * pair_ids[0, 0]
    counts = (first, length - first)
    limits = [
        jnp.maximum(jnp.minimum(highest, count // 2 - 1) - trims[0, 0, cycle], 0)
        for cycle, count in enumerate(counts)
    ]
    return first, [c.astype(jnp.float32) for c in counts], [l.astype(jnp.float32) for l in limits]


def fill_table(axis, chosen, step_waves, facts, blocks, write):
    first, counts, limits = facts
    shape = chosen.shape
    lane = lax.broadcasted_iota(jnp.int32, shape, axis)
    straddle = first // LANES

    def begin(cycle, offset):
        state = unit_circle(chosen, (lane + offset).astype(jnp.float32), counts[cycle])
        kept = chosen <= limits[cycle]
        return tuple(jnp.where(kept, part, 0.0) for part in state)

    steps = step_waves(counts)

    def advance(cycle):
        def body(block, state):
            write(block, state)
            return turn(state, steps[cycle])

        return body

    state = lax.fori_loop(0, straddle, advance(0), begin(0, 0))
    offset = straddle * LANES - first
    later = begin(1, offset)
    before = lane + offset < 0
    write(straddle, tuple(jnp.where(before, old, new) for old, new in zip(state, later)))
    lax.fori_loop(straddle + 1, blocks, advance(1), turn(later, steps[1]))


def ordered_columns(chunk, stride, wavenumbers, raw, columns):
    total = wavenumbers.shape[0]
    raw[...] = jnp.broadcast_to(wavenumbers[...].astype(jnp.float32)[None, :], (LANES, total)).T
    target = 0
    for column in range(2):
        for pair in range(*chunk):
            columns[target:target + STRIP, :] = raw[pl.ds(2 * pair + column, STRIP, stride=stride), :]
            target += STRIP


def forward_kernel(highest, chunk, stride, pair_ids, trims, weights, wavenumbers, grid_hbm, packed_hbm,
                   grid, packed, table, totals, raw, columns, rows, sems):
    length, fields = grid.shape
    width = columns.shape[0]
    arriving = pltpu.make_async_copy(grid_hbm, grid, sems.at[packed.shape[0]])
    arriving.start()
    quarter = width // 2
    facts = cycle_facts(length, highest, pair_ids, trims)
    first, counts, _ = facts
    blocks = -(-length // LANES)
    ordered_columns(chunk, stride, wavenumbers, raw, columns)

    for strip in range(width // STRIP):
        chosen = columns[strip * STRIP:(strip + 1) * STRIP, :]

        def step_waves(counts):
            cycle_lane = lax.broadcasted_iota(jnp.int32, chosen.shape, 1)
            count = jnp.where(cycle_lane == 0, counts[0], counts[1])
            cosine, sine = unit_circle(chosen, float(LANES), count)
            return [
                tuple(jnp.broadcast_to(part[:, c:c + 1], chosen.shape) for part in (cosine, sine))
                for c in range(2)
            ]

        def write(block, state):
            for part in range(2):
                table[
                    part * width + strip * STRIP:part * width + (strip + 1) * STRIP,
                    pl.ds(pl.multiple_of(block * LANES, LANES), LANES),
                ] = state[part].astype(jnp.bfloat16)

        fill_table(1, chosen, step_waves, facts, blocks, write)

    arriving.wait()
    split = -(-(length // 2) // STEP) * STEP
    totals[0] = jnp.zeros(totals.shape[1:], jnp.float32)
    totals[1] = jnp.dot(table[:, split:length], grid[split:, :], preferred_element_type=jnp.float32)
    position = lax.broadcasted_iota(jnp.int32, (STEP, fields), 0)
    for start in range(0, split, STEP):
        block = slice(start, start + STEP)
        data = grid[block, :]
        nothing = jnp.zeros_like(data)

        def add(cycle, data):
            totals[cycle] += jnp.dot(table[:, block], data, preferred_element_type=jnp.float32)

        @pl.when(first >= start + STEP)
        def _():
            add(0, data)

        @pl.when(first <= start)
        def _():
            add(1, data)

        @pl.when((first > start) & (first < start + STEP))
        def _():
            before = position + start < first
            add(0, jnp.where(before, data, nothing))
            add(1, jnp.where(before, nothing, data))

    share = LANES // 4
    leaving = []
    for group in range(fields // share):
        lanes = slice(group * share, (group + 1) * share)
        for cycle in range(2):
            scale = jnp.full((1, LANES), weights[0, 0, cycle]) / counts[cycle]
            joined = jnp.concatenate(
                [totals[cycle, part * quarter:(part + 1) * quarter, lanes] for part in (0, 2, 1, 3)], axis=1
            )
            joined = joined * scale
            for pair in range(quarter // STRIP):
                rows[pl.ds(2 * pair + cycle, STRIP, stride=2 * quarter // STRIP), :] = (
                    joined[pair * STRIP:(pair + 1) * STRIP]
                )
        packed[group] = rows[...].astype(jnp.bfloat16)
        leaving.append(pltpu.make_async_copy(packed.at[group], packed_hbm.at[group], sems.at[group]))
        leaving[-1].start()
    for copy in leaving:
        copy.wait()


def table_kernel(length, highest, stride, pair_ids, trims, wavenumbers, table, raw, columns):
    facts = cycle_facts(length, highest, pair_ids, trims)
    blocks = -(-length // LANES)
    base = 0
    for chunk in CHUNKS:
        width = 2 * STRIP * (chunk[1] - chunk[0])
        ordered_columns(chunk, stride, wavenumbers, raw, columns)
        for tile in range(width // LANES):
            chosen = columns[tile * LANES:(tile + 1) * LANES, :].T

            def step_waves(counts):
                return [
                    tuple(part[:1] for part in unit_circle(chosen[:8], float(LANES), count)) for count in counts
                ]

            def write(block, state):
                for part in range(2):
                    left = base + part * width + tile * LANES
                    table[pl.ds(pl.multiple_of(block * LANES, LANES), LANES), left:left + LANES] = (
                        state[part].astype(jnp.bfloat16)
                    )

            fill_table(0, chosen, step_waves, facts, blocks, write)
        base += 2 * width


def legendre_kernel(start, highest, band, wavenumbers, values, legendre, damping, *refs):
    spectrum, rebuilt = refs[-2:]
    groups, _, degrees, each = legendre.shape

    def matrix(start, count):
        return jnp.concatenate([legendre[group, 0] for group in range(start, start + count)], axis=1)

    rows = (groups * each, LANES)
    sums = jnp.dot(matrix(0, groups), values.reshape(*rows)[...], preferred_element_type=jnp.float32).T
    fields = sums.shape[0] // 2
    pair = band[0] + start + pl.program_id(0)
    first_wave = wavenumbers[2 * pair]
    second_wave = wavenumbers[2 * pair + 1]
    width = damping.shape[1]
    degree = lax.broadcasted_iota(jnp.int32, (1, width), 1)
    kept = degree < highest + 1 - first_wave
    upper = pltpu.roll(damping[...], lax.rem(width - first_wave, width), 1)
    lower = pltpu.roll(damping[...], 1, 1)
    factor = jnp.where(kept, upper[:1], lower[:1])[:, :degrees]
    head = jnp.broadcast_to(kept[:, :degrees], (fields, degrees))
    filtered = (jnp.where(head, sums[:fields], sums[fields:]) * factor).astype(jnp.bfloat16)
    spectrum[0] = filtered
    nothing = jnp.zeros_like(filtered)
    doubled = [
        filtered * jnp.where(wave == 0, 1.0, 2.0).astype(jnp.bfloat16) for wave in (first_wave, second_wave)
    ]
    parts = jnp.concatenate([jnp.where(head, doubled[0], nothing), jnp.where(head, nothing, doubled[1])], axis=0)
    leaving = rebuilt.reshape(*rows)
    for start in range(0, groups, 2):
        products = jnp.dot(parts, matrix(start, 2), preferred_element_type=jnp.float32)
        leaving[start * each:(start + 2) * each, :] = products.astype(jnp.bfloat16).T


def inverse_kernel(chunks, pair_ids, *refs):
    values = refs[:chunks]
    table_hbm, restored, table, rows, factors, sems = refs[chunks:]
    block = pl.program_id(0)
    first = 20 + 4 * pair_ids[0, 0]
    share = LANES // 4

    def arriving(block):
        part = pl.ds(pl.multiple_of(block * INVERSE_BLOCK, 16), INVERSE_BLOCK)
        return pltpu.make_async_copy(table_hbm.at[part, :], table.at[part, :], sems.at[block])

    @pl.when(block == 0)
    def _():
        for one in range(sems.shape[0]):
            arriving(one).start()
        base = 0
        for chunk in values:
            groups, height, _ = chunk.shape
            quarter = height // 2
            for side in range(groups // 4):
                for near in range(4):
                    rows[near, :height] = chunk[4 * side + near].astype(jnp.float32)
                for cycle in range(2):
                    turned = [
                        jnp.concatenate(
                            [
                                rows[near, pl.ds(2 * pair + cycle, STRIP, stride=2 * quarter // STRIP), :]
                                for pair in range(quarter // STRIP)
                            ],
                            axis=0,
                        ).astype(jnp.bfloat16)
                        for near in range(4)
                    ]
                    for part in range(4):
                        source = (0, 2, 1, 3)[part] * share
                        factors[
                            cycle,
                            base + part * quarter:base + (part + 1) * quarter,
                            side * LANES:(side + 1) * LANES,
                        ] = jnp.concatenate([one[:, source:source + share] for one in turned], axis=1)
            base += 4 * quarter

    arriving(block).wait()
    start = pl.multiple_of(block * INVERSE_BLOCK, 16)

    def product(cycle):
        return jnp.dot(
            table[pl.ds(start, INVERSE_BLOCK), :], factors[cycle], preferred_element_type=jnp.float32
        )

    end = start + INVERSE_BLOCK

    @pl.when(end <= first)
    def _():
        restored[...] = product(0).astype(jnp.bfloat16)

    @pl.when(start >= first)
    def _():
        restored[...] = product(1).astype(jnp.bfloat16)

    @pl.when((start < first) & (end > first))
    def _():
        position = start + lax.broadcasted_iota(jnp.int32, restored.shape, 0)
        restored[...] = jnp.where(position < first, product(0), product(1)).astype(jnp.bfloat16)


SMEM = pl.BlockSpec(memory_space=pltpu.SMEM)
VMEM = pl.BlockSpec(memory_space=pltpu.VMEM)


def parameters(*semantics, limit=VMEM_BYTES):
    return pltpu.CompilerParams(dimension_semantics=semantics or None, vmem_limit_bytes=limit)


def forward_call(highest, chunk, stride, pair_ids, trims, weights, wavenumbers, points):
    length, fields = points.shape
    width = 2 * STRIP * (chunk[1] - chunk[0])
    blocks = -(-length // LANES)
    groups = 4 * fields // LANES
    return pl.pallas_call(
        functools.partial(forward_kernel, highest, chunk, stride),
        in_specs=[SMEM, SMEM, SMEM, VMEM, pl.BlockSpec(memory_space=pl.ANY)],
        out_specs=pl.BlockSpec(memory_space=pl.ANY),
        out_shape=jax.ShapeDtypeStruct((groups, width, LANES), jnp.bfloat16),
        scratch_shapes=[
            pltpu.VMEM((length, fields), jnp.bfloat16),
            pltpu.VMEM((groups, width, LANES), jnp.bfloat16),
            pltpu.VMEM((2 * width, blocks * LANES), jnp.bfloat16),
            pltpu.VMEM((2, 2 * width, fields), jnp.float32),
            pltpu.VMEM((wavenumbers.shape[0], LANES), jnp.float32),
            pltpu.VMEM((width, LANES), jnp.float32),
            pltpu.VMEM((width, LANES), jnp.float32),
            pltpu.SemaphoreType.DMA((groups + 1,)),
        ],
        compiler_params=parameters(limit=WHOLE_VMEM_BYTES),
        cost_estimate=pl.CostEstimate(
            flops=2 * length * fields * 2 * width, bytes_accessed=length * fields * 2, transcendentals=0
        ),
        name="forward_dft",
    )(pair_ids, trims, weights, wavenumbers, points)


def table_call(highest, length, stride, pair_ids, trims, wavenumbers):
    blocks = -(-length // LANES)
    total = 2 * wavenumbers.shape[0]
    return pl.pallas_call(
        functools.partial(table_kernel, length, highest, stride),
        in_specs=[SMEM, SMEM, VMEM],
        out_specs=VMEM,
        out_shape=jax.ShapeDtypeStruct((blocks * LANES, total), jnp.bfloat16),
        scratch_shapes=[
            pltpu.VMEM((wavenumbers.shape[0], LANES), jnp.float32),
            pltpu.VMEM((wavenumbers.shape[0], LANES), jnp.float32),
        ],
        compiler_params=parameters(),
        cost_estimate=pl.CostEstimate(flops=8 * length * total, bytes_accessed=2 * length * total, transcendentals=0),
        name="inverse_table",
    )(pair_ids, trims, wavenumbers)


def legendre_call(highest, start, band, wavenumbers, values, gathered, damping, spectrum):
    groups, local_pairs, degrees, each = gathered.shape
    cycles = groups * each
    count = values.shape[1]
    pair_block = pl.BlockSpec((cycles // 2, 1, 2, LANES), lambda q: (0, q, 0, 0))
    fields = LANES // 2
    previous = [] if spectrum is None else [spectrum]
    return pl.pallas_call(
        functools.partial(legendre_kernel, start, highest),
        grid=(count,),
        in_specs=[
            SMEM,
            SMEM,
            pair_block,
            pl.BlockSpec((groups, 1, degrees, each), lambda q: (0, q + start, 0, 0)),
            pl.BlockSpec(damping.shape, lambda q: (0, 0)),
        ]
        + [pl.BlockSpec(memory_space=pl.ANY)] * len(previous),
        out_specs=[
            pl.BlockSpec((1, fields, degrees), lambda q: (q + start, 0, 0)),
            pair_block,
        ],
        out_shape=[
            jax.ShapeDtypeStruct((local_pairs, fields, degrees), jnp.bfloat16),
            jax.ShapeDtypeStruct(values.shape, jnp.bfloat16),
        ],
        input_output_aliases={5: 0} if previous else {},
        compiler_params=parameters("arbitrary", limit=LARGE_VMEM_BYTES),
        cost_estimate=pl.CostEstimate(
            flops=4 * count * cycles * LANES * degrees,
            bytes_accessed=2 * count * cycles * degrees,
            transcendentals=0,
        ),
        name="legendre_both_ways",
    )(band, wavenumbers, values, gathered, damping, *previous)


def inverse_call(length, fields, pair_ids, values, table):
    blocks = -(-length // INVERSE_BLOCK)
    total = table.shape[1]
    return pl.pallas_call(
        functools.partial(inverse_kernel, len(values)),
        grid=(blocks,),
        in_specs=[SMEM]
        + [pl.BlockSpec(one.shape, lambda i: (0, 0, 0)) for one in values]
        + [pl.BlockSpec(memory_space=pl.ANY)],
        out_specs=pl.BlockSpec((INVERSE_BLOCK, fields), lambda i: (i, 0)),
        out_shape=jax.ShapeDtypeStruct((length, fields), jnp.bfloat16),
        scratch_shapes=[
            pltpu.VMEM((blocks * INVERSE_BLOCK, total), jnp.bfloat16),
            pltpu.VMEM((4, max(one.shape[1] for one in values), LANES), jnp.float32),
            pltpu.VMEM((2, total, fields), jnp.bfloat16),
            pltpu.SemaphoreType.DMA((blocks,)),
        ],
        compiler_params=parameters("arbitrary", limit=LARGE_VMEM_BYTES),
        cost_estimate=pl.CostEstimate(
            flops=2 * length * fields * total, bytes_accessed=2 * length * (fields + total), transcendentals=0
        ),
        name="inverse_dft",
    )(pair_ids, *values, table)


def exchange(message):
    return lax.all_to_all(message, ("fld", "band"), split_axis=0, concat_axis=0, tiled=True)


def on_device(grid, pair_ids, trims, weights, wavenumbers, legendre, damping):
    fields, length = grid.shape[2:]
    columns = wavenumbers.shape[0]
    highest = columns - 1
    local_pairs, local_cycles, degrees = legendre.shape
    groups = lax.axis_size("fld")
    bands = lax.axis_size("band")
    gathered = lax.all_gather(legendre.swapaxes(1, 2), "fld")
    points = grid[0, 0].T
    stride = 2 * local_pairs
    padding = -(-degrees // LANES) * LANES - columns
    padded = jnp.broadcast_to(jnp.pad(damping, (0, padding))[None, :], (8, columns + padding))
    band = (lax.axis_index("band") * local_pairs).astype(jnp.int32).reshape(1)

    arrived = []
    for chunk in CHUNKS:
        packed = forward_call(highest, chunk, stride, pair_ids, trims, weights, wavenumbers, points)
        packed, trims = lax.optimization_barrier((packed, trims))
        arrived.append(exchange(packed.reshape(groups * bands, chunk[1] - chunk[0], 2, LANES)))
    table = table_call(highest, length, stride, pair_ids, trims, wavenumbers)
    spectrum = None
    returned = []
    for (start, end), message in zip(CHUNKS, arrived):
        spectrum, rebuilt = legendre_call(
            highest, start, band, wavenumbers, message, gathered, padded, spectrum
        )
        message = exchange(rebuilt)
        returned.append(message.reshape(groups, bands * (end - start) * 2, LANES))
    restored = inverse_call(length, fields, pair_ids, returned, table)
    return (
        spectrum.reshape(local_pairs, 2, fields // groups, degrees),
        restored.T.reshape(1, 1, fields, length),
    )


def solution(mesh):
    placed = (
        P("fld", "band", None, None),
        P("fld", "band"),
        P("fld", "band", None),
        P("fld", "band", None),
        P(),
        P("band", "fld", None),
        P(),
    )
    return jax.shard_map(
        on_device,
        mesh=mesh,
        in_specs=placed,
        out_specs=(P("band", None, "fld", None), P("fld", "band", None, None)),
        check_vma=False,
    )
```

```python
import functools

import jax
import jax.numpy as jnp
from jax import lax
from jax.experimental import pallas as pl
from jax.experimental.pallas import tpu as pltpu
from jax.sharding import PartitionSpec as P

PI = 3.141592653589793
LANES = 128
STEP = 512
INVERSE_BLOCK = 656
STRIP = 64
VMEM_BYTES = 40 * 1024 * 1024
LARGE_VMEM_BYTES = 50_000_000
WHOLE_VMEM_BYTES = 58_000_000
CHUNKS = ((0, 5),)


def unit_circle(waves, points, count):
    inverse = 1.0 / count
    product = waves * points
    residue = product - jnp.round(product * inverse) * count
    half = residue * (inverse * PI)
    square = half * half
    sine = 1.0 / 6227020800.0
    for term in (-1.0 / 39916800.0, 1.0 / 362880.0, -1.0 / 5040.0, 1.0 / 120.0, -1.0 / 6.0, 1.0):
        sine = sine * square + term
    sine = sine * half
    cosine = 1.0 / 479001600.0
    for term in (-1.0 / 3628800.0, 1.0 / 40320.0, -1.0 / 720.0, 1.0 / 24.0, -0.5, 1.0):
        cosine = cosine * square + term
    return cosine * cosine - sine * sine, -2.0 * sine * cosine


def turn(state, step):
    cosine, sine = state
    return cosine * step[0] - sine * step[1], sine * step[0] + cosine * step[1]


def cycle_facts(length, highest, pair_ids, trims):
    first = 20 + 4 * pair_ids[0, 0]
    counts = (first, length - first)
    limits = [
        jnp.maximum(jnp.minimum(highest, count // 2 - 1) - trims[0, 0, cycle], 0)
        for cycle, count in enumerate(counts)
    ]
    return first, [c.astype(jnp.float32) for c in counts], [l.astype(jnp.float32) for l in limits]


def fill_table(axis, chosen, step_waves, facts, blocks, write):
    first, counts, limits = facts
    shape = chosen.shape
    lane = lax.broadcasted_iota(jnp.int32, shape, axis)
    straddle = first // LANES

    def begin(cycle, offset):
        state = unit_circle(chosen, (lane + offset).astype(jnp.float32), counts[cycle])
        kept = chosen <= limits[cycle]
        return tuple(jnp.where(kept, part, 0.0) for part in state)

    steps = step_waves(counts)

    def advance(cycle):
        def body(block, state):
            write(block, state)
            return turn(state, steps[cycle])

        return body

    state = lax.fori_loop(0, straddle, advance(0), begin(0, 0))
    offset = straddle * LANES - first
    later = begin(1, offset)
    before = lane + offset < 0
    write(straddle, tuple(jnp.where(before, old, new) for old, new in zip(state, later)))
    lax.fori_loop(straddle + 1, blocks, advance(1), turn(later, steps[1]))


def ordered_columns(chunk, stride, wavenumbers, raw, columns):
    total = wavenumbers.shape[0]
    raw[...] = jnp.broadcast_to(wavenumbers[...].astype(jnp.float32)[None, :], (LANES, total)).T
    target = 0
    for column in range(2):
        for pair in range(*chunk):
            columns[target:target + STRIP, :] = raw[pl.ds(2 * pair + column, STRIP, stride=stride), :]
            target += STRIP


def forward_kernel(highest, chunk, stride, pair_ids, trims, weights, wavenumbers, grid_hbm, packed_hbm,
                   grid, packed, table, totals, raw, columns, rows, sems):
    length, fields = grid.shape
    width = columns.shape[0]
    arriving = pltpu.make_async_copy(grid_hbm, grid, sems.at[packed.shape[0]])
    arriving.start()
    quarter = width // 2
    facts = cycle_facts(length, highest, pair_ids, trims)
    first, counts, _ = facts
    blocks = -(-length // LANES)
    ordered_columns(chunk, stride, wavenumbers, raw, columns)

    for strip in range(width // STRIP):
        chosen = columns[strip * STRIP:(strip + 1) * STRIP, :]

        def step_waves(counts):
            cycle_lane = lax.broadcasted_iota(jnp.int32, chosen.shape, 1)
            count = jnp.where(cycle_lane == 0, counts[0], counts[1])
            cosine, sine = unit_circle(chosen, float(LANES), count)
            return [
                tuple(jnp.broadcast_to(part[:, c:c + 1], chosen.shape) for part in (cosine, sine))
                for c in range(2)
            ]

        def write(block, state):
            for part in range(2):
                table[
                    part * width + strip * STRIP:part * width + (strip + 1) * STRIP,
                    pl.ds(pl.multiple_of(block * LANES, LANES), LANES),
                ] = state[part].astype(jnp.bfloat16)

        fill_table(1, chosen, step_waves, facts, blocks, write)

    arriving.wait()
    split = -(-(length // 2) // STEP) * STEP
    totals[0] = jnp.zeros(totals.shape[1:], jnp.float32)
    totals[1] = jnp.dot(table[:, split:length], grid[split:, :], preferred_element_type=jnp.float32)
    position = lax.broadcasted_iota(jnp.int32, (STEP, fields), 0)
    for start in range(0, split, STEP):
        block = slice(start, start + STEP)
        data = grid[block, :]
        nothing = jnp.zeros_like(data)

        def add(cycle, data):
            totals[cycle] += jnp.dot(table[:, block], data, preferred_element_type=jnp.float32)

        @pl.when(first >= start + STEP)
        def _():
            add(0, data)

        @pl.when(first <= start)
        def _():
            add(1, data)

        @pl.when((first > start) & (first < start + STEP))
        def _():
            before = position + start < first
            add(0, jnp.where(before, data, nothing))
            add(1, jnp.where(before, nothing, data))

    share = LANES // 4
    leaving = []
    for group in range(fields // share):
        lanes = slice(group * share, (group + 1) * share)
        for cycle in range(2):
            scale = jnp.full((1, LANES), weights[0, 0, cycle]) / counts[cycle]
            joined = jnp.concatenate(
                [totals[cycle, part * quarter:(part + 1) * quarter, lanes] for part in (0, 2, 1, 3)], axis=1
            )
            joined = joined * scale
            for pair in range(quarter // STRIP):
                rows[pl.ds(2 * pair + cycle, STRIP, stride=2 * quarter // STRIP), :] = (
                    joined[pair * STRIP:(pair + 1) * STRIP]
                )
        packed[group] = rows[...].astype(jnp.bfloat16)
        leaving.append(pltpu.make_async_copy(packed.at[group], packed_hbm.at[group], sems.at[group]))
        leaving[-1].start()
    for copy in leaving:
        copy.wait()


def table_kernel(length, highest, stride, pair_ids, trims, wavenumbers, table, raw, columns):
    facts = cycle_facts(length, highest, pair_ids, trims)
    blocks = -(-length // LANES)
    base = 0
    for chunk in CHUNKS:
        width = 2 * STRIP * (chunk[1] - chunk[0])
        ordered_columns(chunk, stride, wavenumbers, raw, columns)
        for tile in range(width // LANES):
            chosen = columns[tile * LANES:(tile + 1) * LANES, :].T

            def step_waves(counts):
                return [
                    tuple(part[:1] for part in unit_circle(chosen[:8], float(LANES), count)) for count in counts
                ]

            def write(block, state):
                for part in range(2):
                    left = base + part * width + tile * LANES
                    table[pl.ds(pl.multiple_of(block * LANES, LANES), LANES), left:left + LANES] = (
                        state[part].astype(jnp.bfloat16)
                    )

            fill_table(0, chosen, step_waves, facts, blocks, write)
        base += 2 * width


def legendre_kernel(start, highest, band, wavenumbers, values, legendre, damping, *refs):
    spectrum, rebuilt = refs[-2:]
    groups, _, degrees, each = legendre.shape

    def matrix(start, count):
        return jnp.concatenate([legendre[group, 0] for group in range(start, start + count)], axis=1)

    rows = (groups * each, LANES)
    sums = jnp.dot(matrix(0, groups), values[0], preferred_element_type=jnp.float32).T
    fields = sums.shape[0] // 2
    pair = band[0] + start + pl.program_id(0)
    first_wave = wavenumbers[2 * pair]
    second_wave = wavenumbers[2 * pair + 1]
    width = damping.shape[1]
    degree = lax.broadcasted_iota(jnp.int32, (1, width), 1)
    kept = degree < highest + 1 - first_wave
    upper = pltpu.roll(damping[...], lax.rem(width - first_wave, width), 1)
    lower = pltpu.roll(damping[...], 1, 1)
    factor = jnp.where(kept, upper[:1], lower[:1])[:, :degrees]
    head = jnp.broadcast_to(kept[:, :degrees], (fields, degrees))
    filtered = (jnp.where(head, sums[:fields], sums[fields:]) * factor).astype(jnp.bfloat16)
    spectrum[0] = filtered
    nothing = jnp.zeros_like(filtered)
    doubled = [
        filtered * jnp.where(wave == 0, 1.0, 2.0).astype(jnp.bfloat16) for wave in (first_wave, second_wave)
    ]
    parts = jnp.concatenate([jnp.where(head, doubled[0], nothing), jnp.where(head, nothing, doubled[1])], axis=0)
    leaving = rebuilt.reshape(*rows)
    for start in range(0, groups, 2):
        products = jnp.dot(parts, matrix(start, 2), preferred_element_type=jnp.float32)
        leaving[start * each:(start + 2) * each, :] = products.astype(jnp.bfloat16).T


def inverse_kernel(chunks, pair_ids, *refs):
    values = refs[:chunks]
    table_hbm, restored, table, rows, factors, sems = refs[chunks:]
    block = pl.program_id(0)
    first = 20 + 4 * pair_ids[0, 0]
    share = LANES // 4

    def arriving(block):
        part = pl.ds(pl.multiple_of(block * INVERSE_BLOCK, 16), INVERSE_BLOCK)
        return pltpu.make_async_copy(table_hbm.at[part, :], table.at[part, :], sems.at[block])

    @pl.when(block == 0)
    def _():
        for one in range(sems.shape[0]):
            arriving(one).start()
        base = 0
        for chunk in values:
            groups, height, _ = chunk.shape
            quarter = height // 2
            for side in range(groups // 4):
                for near in range(4):
                    rows[near, :height] = chunk[4 * side + near].astype(jnp.float32)
                for cycle in range(2):
                    turned = [
                        jnp.concatenate(
                            [
                                rows[near, pl.ds(2 * pair + cycle, STRIP, stride=2 * quarter // STRIP), :]
                                for pair in range(quarter // STRIP)
                            ],
                            axis=0,
                        ).astype(jnp.bfloat16)
                        for near in range(4)
                    ]
                    for part in range(4):
                        source = (0, 2, 1, 3)[part] * share
                        factors[
                            cycle,
                            base + part * quarter:base + (part + 1) * quarter,
                            side * LANES:(side + 1) * LANES,
                        ] = jnp.concatenate([one[:, source:source + share] for one in turned], axis=1)
            base += 4 * quarter

    arriving(block).wait()
    start = pl.multiple_of(block * INVERSE_BLOCK, 16)

    def product(cycle):
        return jnp.dot(
            table[pl.ds(start, INVERSE_BLOCK), :], factors[cycle], preferred_element_type=jnp.float32
        )

    end = start + INVERSE_BLOCK

    @pl.when(end <= first)
    def _():
        restored[...] = product(0).astype(jnp.bfloat16)

    @pl.when(start >= first)
    def _():
        restored[...] = product(1).astype(jnp.bfloat16)

    @pl.when((start < first) & (end > first))
    def _():
        position = start + lax.broadcasted_iota(jnp.int32, restored.shape, 0)
        restored[...] = jnp.where(position < first, product(0), product(1)).astype(jnp.bfloat16)


SMEM = pl.BlockSpec(memory_space=pltpu.SMEM)
VMEM = pl.BlockSpec(memory_space=pltpu.VMEM)


def parameters(*semantics, limit=VMEM_BYTES):
    return pltpu.CompilerParams(dimension_semantics=semantics or None, vmem_limit_bytes=limit)


def forward_call(highest, chunk, stride, pair_ids, trims, weights, wavenumbers, points):
    length, fields = points.shape
    width = 2 * STRIP * (chunk[1] - chunk[0])
    blocks = -(-length // LANES)
    groups = 4 * fields // LANES
    return pl.pallas_call(
        functools.partial(forward_kernel, highest, chunk, stride),
        in_specs=[SMEM, SMEM, SMEM, VMEM, pl.BlockSpec(memory_space=pl.ANY)],
        out_specs=pl.BlockSpec(memory_space=pl.ANY),
        out_shape=jax.ShapeDtypeStruct((groups, width, LANES), jnp.bfloat16),
        scratch_shapes=[
            pltpu.VMEM((length, fields), jnp.bfloat16),
            pltpu.VMEM((groups, width, LANES), jnp.bfloat16),
            pltpu.VMEM((2 * width, blocks * LANES), jnp.bfloat16),
            pltpu.VMEM((2, 2 * width, fields), jnp.float32),
            pltpu.VMEM((wavenumbers.shape[0], LANES), jnp.float32),
            pltpu.VMEM((width, LANES), jnp.float32),
            pltpu.VMEM((width, LANES), jnp.float32),
            pltpu.SemaphoreType.DMA((groups + 1,)),
        ],
        compiler_params=parameters(limit=WHOLE_VMEM_BYTES),
        cost_estimate=pl.CostEstimate(
            flops=2 * length * fields * 2 * width, bytes_accessed=length * fields * 2, transcendentals=0
        ),
        name="forward_dft",
    )(pair_ids, trims, weights, wavenumbers, points)


def table_call(highest, length, stride, pair_ids, trims, wavenumbers):
    blocks = -(-length // LANES)
    total = 2 * wavenumbers.shape[0]
    return pl.pallas_call(
        functools.partial(table_kernel, length, highest, stride),
        in_specs=[SMEM, SMEM, VMEM],
        out_specs=VMEM,
        out_shape=jax.ShapeDtypeStruct((blocks * LANES, total), jnp.bfloat16),
        scratch_shapes=[
            pltpu.VMEM((wavenumbers.shape[0], LANES), jnp.float32),
            pltpu.VMEM((wavenumbers.shape[0], LANES), jnp.float32),
        ],
        compiler_params=parameters(),
        cost_estimate=pl.CostEstimate(flops=8 * length * total, bytes_accessed=2 * length * total, transcendentals=0),
        name="inverse_table",
    )(pair_ids, trims, wavenumbers)


def legendre_call(highest, start, band, wavenumbers, values, gathered, damping, spectrum):
    groups, local_pairs, degrees, each = gathered.shape
    count, cycles, _ = values.shape
    pair_block = pl.BlockSpec((cycles // 2, 1, 2, LANES), lambda q: (0, q, 0, 0))
    fields = LANES // 2
    previous = [] if spectrum is None else [spectrum]
    return pl.pallas_call(
        functools.partial(legendre_kernel, start, highest),
        grid=(count,),
        in_specs=[
            SMEM,
            SMEM,
            pl.BlockSpec((1, cycles, LANES), lambda q: (q, 0, 0)),
            pl.BlockSpec((groups, 1, degrees, each), lambda q: (0, q + start, 0, 0)),
            pl.BlockSpec(damping.shape, lambda q: (0, 0)),
        ]
        + [pl.BlockSpec(memory_space=pl.ANY)] * len(previous),
        out_specs=[
            pl.BlockSpec((1, fields, degrees), lambda q: (q + start, 0, 0)),
            pair_block,
        ],
        out_shape=[
            jax.ShapeDtypeStruct((local_pairs, fields, degrees), jnp.bfloat16),
            jax.ShapeDtypeStruct((cycles // 2, count, 2, LANES), jnp.bfloat16),
        ],
        input_output_aliases={5: 0} if previous else {},
        compiler_params=parameters("arbitrary", limit=LARGE_VMEM_BYTES),
        cost_estimate=pl.CostEstimate(
            flops=4 * count * cycles * LANES * degrees,
            bytes_accessed=2 * count * cycles * degrees,
            transcendentals=0,
        ),
        name="legendre_both_ways",
    )(band, wavenumbers, values, gathered, damping, *previous)


def inverse_call(length, fields, pair_ids, values, table):
    blocks = -(-length // INVERSE_BLOCK)
    total = table.shape[1]
    return pl.pallas_call(
        functools.partial(inverse_kernel, len(values)),
        grid=(blocks,),
        in_specs=[SMEM]
        + [pl.BlockSpec(one.shape, lambda i: (0, 0, 0)) for one in values]
        + [pl.BlockSpec(memory_space=pl.ANY)],
        out_specs=pl.BlockSpec((INVERSE_BLOCK, fields), lambda i: (i, 0)),
        out_shape=jax.ShapeDtypeStruct((length, fields), jnp.bfloat16),
        scratch_shapes=[
            pltpu.VMEM((blocks * INVERSE_BLOCK, total), jnp.bfloat16),
            pltpu.VMEM((4, max(one.shape[1] for one in values), LANES), jnp.float32),
            pltpu.VMEM((2, total, fields), jnp.bfloat16),
            pltpu.SemaphoreType.DMA((blocks,)),
        ],
        compiler_params=parameters("arbitrary", limit=LARGE_VMEM_BYTES),
        cost_estimate=pl.CostEstimate(
            flops=2 * length * fields * total, bytes_accessed=2 * length * (fields + total), transcendentals=0
        ),
        name="inverse_dft",
    )(pair_ids, *values, table)


def exchange(message):
    return lax.all_to_all(message, ("fld", "band"), split_axis=0, concat_axis=0, tiled=True)


def on_device(grid, pair_ids, trims, weights, wavenumbers, legendre, damping):
    fields, length = grid.shape[2:]
    columns = wavenumbers.shape[0]
    highest = columns - 1
    local_pairs, local_cycles, degrees = legendre.shape
    groups = lax.axis_size("fld")
    bands = lax.axis_size("band")
    gathered = lax.all_gather(legendre.swapaxes(1, 2), "fld")
    points = grid[0, 0].T
    stride = 2 * local_pairs
    padding = -(-degrees // LANES) * LANES - columns
    padded = jnp.broadcast_to(jnp.pad(damping, (0, padding))[None, :], (8, columns + padding))
    band = (lax.axis_index("band") * local_pairs).astype(jnp.int32).reshape(1)

    arrived = []
    for chunk in CHUNKS:
        packed = forward_call(highest, chunk, stride, pair_ids, trims, weights, wavenumbers, points)
        packed, trims = lax.optimization_barrier((packed, trims))
        arrived.append(exchange(packed.reshape(groups * bands, chunk[1] - chunk[0], 2, LANES)))
    table = table_call(highest, length, stride, pair_ids, trims, wavenumbers)
    spectrum = None
    returned = []
    for (start, end), message in zip(CHUNKS, arrived):
        values = message.transpose(1, 0, 2, 3).reshape(end - start, groups * local_cycles, LANES)
        spectrum, rebuilt = legendre_call(
            highest, start, band, wavenumbers, values, gathered, padded, spectrum
        )
        message = exchange(rebuilt)
        returned.append(message.reshape(groups, bands * (end - start) * 2, LANES))
    restored = inverse_call(length, fields, pair_ids, returned, table)
    return (
        spectrum.reshape(local_pairs, 2, fields // groups, degrees),
        restored.T.reshape(1, 1, fields, length),
    )


def solution(mesh):
    placed = (
        P("fld", "band", None, None),
        P("fld", "band"),
        P("fld", "band", None),
        P("fld", "band", None),
        P(),
        P("band", "fld", None),
        P(),
    )
    return jax.shard_map(
        on_device,
        mesh=mesh,
        in_specs=placed,
        out_specs=(P("band", None, "fld", None), P("fld", "band", None, None)),
        check_vma=False,
    )
```

```python
import functools

import jax
import jax.numpy as jnp
from jax import lax
from jax.experimental import pallas as pl
from jax.experimental.pallas import tpu as pltpu
from jax.sharding import PartitionSpec as P

PI = 3.141592653589793
LANES = 128
STEP = 512
INVERSE_BLOCK = 656
STRIP = 64
VMEM_BYTES = 40 * 1024 * 1024
LARGE_VMEM_BYTES = 50_000_000
WHOLE_VMEM_BYTES = 58_000_000
CHUNKS = ((0, 5),)


def unit_circle(waves, points, count):
    inverse = 1.0 / count
    product = waves * points
    residue = product - jnp.round(product * inverse) * count
    half = residue * (inverse * PI)
    square = half * half
    sine = 1.0 / 6227020800.0
    for term in (-1.0 / 39916800.0, 1.0 / 362880.0, -1.0 / 5040.0, 1.0 / 120.0, -1.0 / 6.0, 1.0):
        sine = sine * square + term
    sine = sine * half
    cosine = 1.0 / 479001600.0
    for term in (-1.0 / 3628800.0, 1.0 / 40320.0, -1.0 / 720.0, 1.0 / 24.0, -0.5, 1.0):
        cosine = cosine * square + term
    return cosine * cosine - sine * sine, -2.0 * sine * cosine


def turn(state, step):
    cosine, sine = state
    return cosine * step[0] - sine * step[1], sine * step[0] + cosine * step[1]


def cycle_facts(length, highest, pair_ids, trims):
    first = 20 + 4 * pair_ids[0, 0]
    counts = (first, length - first)
    limits = [
        jnp.maximum(jnp.minimum(highest, count // 2 - 1) - trims[0, 0, cycle], 0)
        for cycle, count in enumerate(counts)
    ]
    return first, [c.astype(jnp.float32) for c in counts], [l.astype(jnp.float32) for l in limits]


def fill_table(axis, chosen, step_waves, facts, blocks, write):
    first, counts, limits = facts
    shape = chosen.shape
    lane = lax.broadcasted_iota(jnp.int32, shape, axis)
    straddle = first // LANES

    def begin(cycle, offset):
        state = unit_circle(chosen, (lane + offset).astype(jnp.float32), counts[cycle])
        kept = chosen <= limits[cycle]
        return tuple(jnp.where(kept, part, 0.0) for part in state)

    steps = step_waves(counts)

    def advance(cycle):
        def body(block, state):
            write(block, state)
            return turn(state, steps[cycle])

        return body

    state = lax.fori_loop(0, straddle, advance(0), begin(0, 0))
    offset = straddle * LANES - first
    later = begin(1, offset)
    before = lane + offset < 0
    write(straddle, tuple(jnp.where(before, old, new) for old, new in zip(state, later)))
    lax.fori_loop(straddle + 1, blocks, advance(1), turn(later, steps[1]))


def ordered_columns(chunk, stride, wavenumbers, raw, columns):
    total = wavenumbers.shape[0]
    raw[...] = jnp.broadcast_to(wavenumbers[...].astype(jnp.float32)[None, :], (LANES, total)).T
    target = 0
    for column in range(2):
        for pair in range(*chunk):
            columns[target:target + STRIP, :] = raw[pl.ds(2 * pair + column, STRIP, stride=stride), :]
            target += STRIP


def forward_kernel(highest, chunk, stride, pair_ids, trims, weights, wavenumbers, grid_hbm, packed_hbm,
                   grid, packed, table, totals, raw, columns, rows, sems):
    length, fields = grid.shape
    width = columns.shape[0]
    arriving = pltpu.make_async_copy(grid_hbm, grid, sems.at[packed.shape[0]])
    arriving.start()
    quarter = width // 2
    facts = cycle_facts(length, highest, pair_ids, trims)
    first, counts, _ = facts
    blocks = -(-length // LANES)
    ordered_columns(chunk, stride, wavenumbers, raw, columns)

    for strip in range(width // STRIP):
        chosen = columns[strip * STRIP:(strip + 1) * STRIP, :]

        def step_waves(counts):
            cycle_lane = lax.broadcasted_iota(jnp.int32, chosen.shape, 1)
            count = jnp.where(cycle_lane == 0, counts[0], counts[1])
            cosine, sine = unit_circle(chosen, float(LANES), count)
            return [
                tuple(jnp.broadcast_to(part[:, c:c + 1], chosen.shape) for part in (cosine, sine))
                for c in range(2)
            ]

        def write(block, state):
            for part in range(2):
                table[
                    part * width + strip * STRIP:part * width + (strip + 1) * STRIP,
                    pl.ds(pl.multiple_of(block * LANES, LANES), LANES),
                ] = state[part].astype(jnp.bfloat16)

        fill_table(1, chosen, step_waves, facts, blocks, write)

    arriving.wait()
    split = -(-(length // 2) // STEP) * STEP
    totals[0] = jnp.zeros(totals.shape[1:], jnp.float32)
    totals[1] = jnp.dot(table[:, split:length], grid[split:, :], preferred_element_type=jnp.float32)
    position = lax.broadcasted_iota(jnp.int32, (STEP, fields), 0)
    for start in range(0, split, STEP):
        block = slice(start, start + STEP)
        data = grid[block, :]
        nothing = jnp.zeros_like(data)

        def add(cycle, data):
            totals[cycle] += jnp.dot(table[:, block], data, preferred_element_type=jnp.float32)

        @pl.when(first >= start + STEP)
        def _():
            add(0, data)

        @pl.when(first <= start)
        def _():
            add(1, data)

        @pl.when((first > start) & (first < start + STEP))
        def _():
            before = position + start < first
            add(0, jnp.where(before, data, nothing))
            add(1, jnp.where(before, nothing, data))

    share = LANES // 4
    leaving = []
    for group in range(fields // share):
        lanes = slice(group * share, (group + 1) * share)
        for cycle in range(2):
            scale = jnp.full((1, LANES), weights[0, 0, cycle]) / counts[cycle]
            joined = jnp.concatenate(
                [totals[cycle, part * quarter:(part + 1) * quarter, lanes] for part in (0, 2, 1, 3)], axis=1
            )
            joined = joined * scale
            for pair in range(quarter // STRIP):
                rows[pl.ds(2 * pair + cycle, STRIP, stride=2 * quarter // STRIP), :] = (
                    joined[pair * STRIP:(pair + 1) * STRIP]
                )
        packed[group] = rows[...].astype(jnp.bfloat16)
        leaving.append(pltpu.make_async_copy(packed.at[group], packed_hbm.at[group], sems.at[group]))
        leaving[-1].start()
    for copy in leaving:
        copy.wait()


def table_kernel(length, highest, stride, pair_ids, trims, wavenumbers, table, raw, columns):
    facts = cycle_facts(length, highest, pair_ids, trims)
    blocks = -(-length // LANES)
    base = 0
    for chunk in CHUNKS:
        width = 2 * STRIP * (chunk[1] - chunk[0])
        ordered_columns(chunk, stride, wavenumbers, raw, columns)
        for tile in range(width // LANES):
            chosen = columns[tile * LANES:(tile + 1) * LANES, :].T

            def step_waves(counts):
                return [
                    tuple(part[:1] for part in unit_circle(chosen[:8], float(LANES), count)) for count in counts
                ]

            def write(block, state):
                for part in range(2):
                    left = base + part * width + tile * LANES
                    table[pl.ds(pl.multiple_of(block * LANES, LANES), LANES), left:left + LANES] = (
                        state[part].astype(jnp.bfloat16)
                    )

            fill_table(0, chosen, step_waves, facts, blocks, write)
        base += 2 * width


def legendre_kernel(start, highest, band, wavenumbers, values, legendre, damping, *refs):
    spectrum, rebuilt = refs[-2:]
    groups, _, degrees, each = legendre.shape

    def matrix(start, count):
        return jnp.concatenate([legendre[group, 0] for group in range(start, start + count)], axis=1)

    rows = (groups * each, LANES)
    sums = jnp.dot(matrix(0, groups), values[0], preferred_element_type=jnp.float32).T
    fields = sums.shape[0] // 2
    pair = band[0] + start + pl.program_id(0)
    first_wave = wavenumbers[2 * pair]
    second_wave = wavenumbers[2 * pair + 1]
    width = damping.shape[1]
    degree = lax.broadcasted_iota(jnp.int32, (1, width), 1)
    kept = degree < highest + 1 - first_wave
    upper = pltpu.roll(damping[...], lax.rem(width - first_wave, width), 1)
    lower = pltpu.roll(damping[...], 1, 1)
    factor = jnp.where(kept, upper[:1], lower[:1])[:, :degrees]
    head = jnp.broadcast_to(kept[:, :degrees], (fields, degrees))
    filtered = (jnp.where(head, sums[:fields], sums[fields:]) * factor).astype(jnp.bfloat16)
    spectrum[0] = filtered
    nothing = jnp.zeros_like(filtered)
    doubled = [
        filtered * jnp.where(wave == 0, 1.0, 2.0).astype(jnp.bfloat16) for wave in (first_wave, second_wave)
    ]
    parts = jnp.concatenate([jnp.where(head, doubled[0], nothing), jnp.where(head, nothing, doubled[1])], axis=0)
    leaving = rebuilt.reshape(*rows)
    for start in range(0, groups, 2):
        products = jnp.dot(parts, matrix(start, 2), preferred_element_type=jnp.float32)
        leaving[start * each:(start + 2) * each, :] = products.astype(jnp.bfloat16).T


def inverse_kernel(chunks, pair_ids, *refs):
    values = refs[:chunks]
    table_hbm, restored, table, messages, rows, factors, sems, message_sems = refs[chunks:]
    block = pl.program_id(0)
    first = 20 + 4 * pair_ids[0, 0]
    share = LANES // 4

    def arriving(block):
        part = pl.ds(pl.multiple_of(block * INVERSE_BLOCK, 16), INVERSE_BLOCK)
        return pltpu.make_async_copy(table_hbm.at[part, :], table.at[part, :], sems.at[block])

    @pl.when(block == 0)
    def _():
        base = 0
        for chunk in values:
            groups, height, _ = chunk.shape
            quarter = height // 2
            copies = [
                pltpu.make_async_copy(chunk.at[group], messages.at[group], message_sems.at[group])
                for group in range(groups)
            ]
            for copy in copies:
                copy.start()
            if base == 0:
                for one in range(sems.shape[0]):
                    arriving(one).start()
            for side in range(groups // 4):
                for near in range(4):
                    copies[4 * side + near].wait()
                    rows[near, :height] = messages[4 * side + near].astype(jnp.float32)
                for cycle in range(2):
                    turned = [
                        jnp.concatenate(
                            [
                                rows[near, pl.ds(2 * pair + cycle, STRIP, stride=2 * quarter // STRIP), :]
                                for pair in range(quarter // STRIP)
                            ],
                            axis=0,
                        ).astype(jnp.bfloat16)
                        for near in range(4)
                    ]
                    for part in range(4):
                        source = (0, 2, 1, 3)[part] * share
                        factors[
                            cycle,
                            base + part * quarter:base + (part + 1) * quarter,
                            side * LANES:(side + 1) * LANES,
                        ] = jnp.concatenate([one[:, source:source + share] for one in turned], axis=1)
            base += 4 * quarter

    arriving(block).wait()
    start = pl.multiple_of(block * INVERSE_BLOCK, 16)

    def product(cycle):
        return jnp.dot(
            table[pl.ds(start, INVERSE_BLOCK), :], factors[cycle], preferred_element_type=jnp.float32
        )

    end = start + INVERSE_BLOCK

    @pl.when(end <= first)
    def _():
        restored[...] = product(0).astype(jnp.bfloat16)

    @pl.when(start >= first)
    def _():
        restored[...] = product(1).astype(jnp.bfloat16)

    @pl.when((start < first) & (end > first))
    def _():
        position = start + lax.broadcasted_iota(jnp.int32, restored.shape, 0)
        restored[...] = jnp.where(position < first, product(0), product(1)).astype(jnp.bfloat16)


SMEM = pl.BlockSpec(memory_space=pltpu.SMEM)
VMEM = pl.BlockSpec(memory_space=pltpu.VMEM)


def parameters(*semantics, limit=VMEM_BYTES):
    return pltpu.CompilerParams(dimension_semantics=semantics or None, vmem_limit_bytes=limit)


def forward_call(highest, chunk, stride, pair_ids, trims, weights, wavenumbers, points):
    length, fields = points.shape
    width = 2 * STRIP * (chunk[1] - chunk[0])
    blocks = -(-length // LANES)
    groups = 4 * fields // LANES
    return pl.pallas_call(
        functools.partial(forward_kernel, highest, chunk, stride),
        in_specs=[SMEM, SMEM, SMEM, VMEM, pl.BlockSpec(memory_space=pl.ANY)],
        out_specs=pl.BlockSpec(memory_space=pl.ANY),
        out_shape=jax.ShapeDtypeStruct((groups, width, LANES), jnp.bfloat16),
        scratch_shapes=[
            pltpu.VMEM((length, fields), jnp.bfloat16),
            pltpu.VMEM((groups, width, LANES), jnp.bfloat16),
            pltpu.VMEM((2 * width, blocks * LANES), jnp.bfloat16),
            pltpu.VMEM((2, 2 * width, fields), jnp.float32),
            pltpu.VMEM((wavenumbers.shape[0], LANES), jnp.float32),
            pltpu.VMEM((width, LANES), jnp.float32),
            pltpu.VMEM((width, LANES), jnp.float32),
            pltpu.SemaphoreType.DMA((groups + 1,)),
        ],
        compiler_params=parameters(limit=WHOLE_VMEM_BYTES),
        cost_estimate=pl.CostEstimate(
            flops=2 * length * fields * 2 * width, bytes_accessed=length * fields * 2, transcendentals=0
        ),
        name="forward_dft",
    )(pair_ids, trims, weights, wavenumbers, points)


def table_call(highest, length, stride, pair_ids, trims, wavenumbers):
    blocks = -(-length // LANES)
    total = 2 * wavenumbers.shape[0]
    return pl.pallas_call(
        functools.partial(table_kernel, length, highest, stride),
        in_specs=[SMEM, SMEM, VMEM],
        out_specs=VMEM,
        out_shape=jax.ShapeDtypeStruct((blocks * LANES, total), jnp.bfloat16),
        scratch_shapes=[
            pltpu.VMEM((wavenumbers.shape[0], LANES), jnp.float32),
            pltpu.VMEM((wavenumbers.shape[0], LANES), jnp.float32),
        ],
        compiler_params=parameters(),
        cost_estimate=pl.CostEstimate(flops=8 * length * total, bytes_accessed=2 * length * total, transcendentals=0),
        name="inverse_table",
    )(pair_ids, trims, wavenumbers)


def legendre_call(highest, start, band, wavenumbers, values, gathered, damping, spectrum):
    groups, local_pairs, degrees, each = gathered.shape
    count, cycles, _ = values.shape
    pair_block = pl.BlockSpec((cycles // 2, 1, 2, LANES), lambda q: (0, q, 0, 0))
    fields = LANES // 2
    previous = [] if spectrum is None else [spectrum]
    return pl.pallas_call(
        functools.partial(legendre_kernel, start, highest),
        grid=(count,),
        in_specs=[
            SMEM,
            SMEM,
            pl.BlockSpec((1, cycles, LANES), lambda q: (q, 0, 0)),
            pl.BlockSpec((groups, 1, degrees, each), lambda q: (0, q + start, 0, 0)),
            pl.BlockSpec(damping.shape, lambda q: (0, 0)),
        ]
        + [pl.BlockSpec(memory_space=pl.ANY)] * len(previous),
        out_specs=[
            pl.BlockSpec((1, fields, degrees), lambda q: (q + start, 0, 0)),
            pair_block,
        ],
        out_shape=[
            jax.ShapeDtypeStruct((local_pairs, fields, degrees), jnp.bfloat16),
            jax.ShapeDtypeStruct((cycles // 2, count, 2, LANES), jnp.bfloat16),
        ],
        input_output_aliases={5: 0} if previous else {},
        compiler_params=parameters("arbitrary", limit=LARGE_VMEM_BYTES),
        cost_estimate=pl.CostEstimate(
            flops=4 * count * cycles * LANES * degrees,
            bytes_accessed=2 * count * cycles * degrees,
            transcendentals=0,
        ),
        name="legendre_both_ways",
    )(band, wavenumbers, values, gathered, damping, *previous)


def inverse_call(length, fields, pair_ids, values, table):
    blocks = -(-length // INVERSE_BLOCK)
    total = table.shape[1]
    return pl.pallas_call(
        functools.partial(inverse_kernel, len(values)),
        grid=(blocks,),
        in_specs=[SMEM]
        + [pl.BlockSpec(memory_space=pl.ANY)] * len(values)
        + [pl.BlockSpec(memory_space=pl.ANY)],
        out_specs=pl.BlockSpec((INVERSE_BLOCK, fields), lambda i: (i, 0)),
        out_shape=jax.ShapeDtypeStruct((length, fields), jnp.bfloat16),
        scratch_shapes=[
            pltpu.VMEM((blocks * INVERSE_BLOCK, total), jnp.bfloat16),
            pltpu.VMEM(values[0].shape, jnp.bfloat16),
            pltpu.VMEM((4, max(one.shape[1] for one in values), LANES), jnp.float32),
            pltpu.VMEM((2, total, fields), jnp.bfloat16),
            pltpu.SemaphoreType.DMA((blocks,)),
            pltpu.SemaphoreType.DMA((values[0].shape[0],)),
        ],
        compiler_params=parameters("arbitrary", limit=LARGE_VMEM_BYTES),
        cost_estimate=pl.CostEstimate(
            flops=2 * length * fields * total, bytes_accessed=2 * length * (fields + total), transcendentals=0
        ),
        name="inverse_dft",
    )(pair_ids, *values, table)


def exchange(message):
    return lax.all_to_all(message, ("fld", "band"), split_axis=0, concat_axis=0, tiled=True)


def on_device(grid, pair_ids, trims, weights, wavenumbers, legendre, damping):
    fields, length = grid.shape[2:]
    columns = wavenumbers.shape[0]
    highest = columns - 1
    local_pairs, local_cycles, degrees = legendre.shape
    groups = lax.axis_size("fld")
    bands = lax.axis_size("band")
    gathered = lax.all_gather(legendre.swapaxes(1, 2), "fld")
    points = grid[0, 0].T
    stride = 2 * local_pairs
    padding = -(-degrees // LANES) * LANES - columns
    padded = jnp.broadcast_to(jnp.pad(damping, (0, padding))[None, :], (8, columns + padding))
    band = (lax.axis_index("band") * local_pairs).astype(jnp.int32).reshape(1)

    arrived = []
    for chunk in CHUNKS:
        packed = forward_call(highest, chunk, stride, pair_ids, trims, weights, wavenumbers, points)
        packed, trims = lax.optimization_barrier((packed, trims))
        arrived.append(exchange(packed.reshape(groups * bands, chunk[1] - chunk[0], 2, LANES)))
    table = table_call(highest, length, stride, pair_ids, trims, wavenumbers)
    spectrum = None
    returned = []
    for (start, end), message in zip(CHUNKS, arrived):
        values = message.transpose(1, 0, 2, 3).reshape(end - start, groups * local_cycles, LANES)
        spectrum, rebuilt = legendre_call(
            highest, start, band, wavenumbers, values, gathered, padded, spectrum
        )
        message = exchange(rebuilt)
        returned.append(message.reshape(groups, bands * (end - start) * 2, LANES))
    restored = inverse_call(length, fields, pair_ids, returned, table)
    return (
        spectrum.reshape(local_pairs, 2, fields // groups, degrees),
        restored.T.reshape(1, 1, fields, length),
    )


def solution(mesh):
    placed = (
        P("fld", "band", None, None),
        P("fld", "band"),
        P("fld", "band", None),
        P("fld", "band", None),
        P(),
        P("band", "fld", None),
        P(),
    )
    return jax.shard_map(
        on_device,
        mesh=mesh,
        in_specs=placed,
        out_specs=(P("band", None, "fld", None), P("fld", "band", None, None)),
        check_vma=False,
    )
```
